32 devices in a mesh: dp: 16 (over z, x, core), tensor: 2 (over y).
Axes of the slice: x: 2, y: 2, z: 4, core: 2. Of those that a mesh axis runs over, the one named last changes fastest.
Arguments:
- tokens: bfloat16 [49152, 1024], P(('dp', 'tensor')), may hold values from -6 to 6
- seq_lengths: int32 [16, 3], P('dp'), may hold values from 0 to 1024, as said below
- first_gain: float32 [1024], replicated, may hold values from 0.5 to 1.5
- mix_weight: bfloat16 [1024, 6144], P(None, 'tensor'), may hold values from -0.1875 to 0.1875
- rate_weight: bfloat16 [1024, 16], P(None, 'tensor'), may hold values from -0.1875 to 0.1875
- conv_weight: float32 [4, 4096], P(None, 'tensor'), may hold values from -3 to 3
- decay_log: float32 [8], P('tensor'), may hold values from -4 to 1
- decay_bias: float32 [8], P('tensor'), may hold values from -4 to 1
- out_gain: float32 [256], replicated, may hold values from 0.5 to 1.5
- out_weight: bfloat16 [2048, 1024], P('tensor'), may hold values from -0.375 to 0.375
- second_gain: float32 [1024], replicated, may hold values from 0.5 to 1.5
- gate_weight: bfloat16 [1024, 2816], P(None, 'tensor'), may hold values from -0.1875 to 0.1875
- up_weight: bfloat16 [1024, 2816], P(None, 'tensor'), may hold values from -0.1875 to 0.1875
- down_weight: bfloat16 [2816, 1024], P('tensor'), may hold values from -0.109375 to 0.109375
- cotangent: bfloat16 [49152, 1024], P(('dp', 'tensor')), may hold values from -6 to 6
Outputs:
- block_out: bfloat16 [49152, 1024], P(('dp', 'tensor'))
- tokens_grad: bfloat16 [49152, 1024], P(('dp', 'tensor'))
- grad_first_gain: float32 [1024], replicated
- grad_mix_weight: float32 [1024, 6144], P(None, 'tensor')
- grad_rate_weight: float32 [1024, 16], P(None, 'tensor')
- grad_conv_weight: float32 [4, 4096], P(None, 'tensor')
- grad_decay_log: float32 [8], P('tensor')
- grad_decay_bias: float32 [8], P('tensor')
- grad_out_gain: float32 [256], replicated
- grad_out_weight: float32 [2048, 1024], P('tensor')
- grad_second_gain: float32 [1024], replicated
- grad_gate_weight: float32 [1024, 2816], P(None, 'tensor')
- grad_up_weight: float32 [1024, 2816], P(None, 'tensor')
- grad_down_weight: float32 [2816, 1024], P('tensor')
The draws below stay inside these ranges and needn't reach their ends.
Inputs may be any that keep to these rules, and one draw needn't show every extreme that they name: `seq_lengths`: row g lists the lengths of the sequences packed in order from the first of group g's 3072 slots; its nonzero entries come first, two or more of them, each from 256 to 1024, and the rest are 0. In every draw one row holds 3 sequences of 1024 tokens and fills its group.
All inputs are finite; a program needn't handle non-finite values.
Results may differ from the reference program's by a relative error of at most 0.019.
Values may be sent and summed in bfloat16 or wider, within the bound.
No kernel may reach another device: no remote copies, remote signals or barrier semaphores. Data moves between devices by JAX's collectives and lax.ppermute only.
A program may use at most 640 MiB of HBM per device.

```python
from functools import partial
import jax
import jax.numpy as jnp
from jax import lax

D = 1024
H = 8
DK = 128
DV = 256
FF = 2816
CONV = 4
SPAN = 64
SEQ_MAX = 1024
SEQ_MIN = 256
NSEQ = 3
GROUPS = 16
TOKENS = 49152


def draw_seq_lengths(key, part):
    key = jax.random.fold_in(key, 7)
    first, second, third = jax.random.split(key, 3)
    lengths = jax.random.randint(first, (GROUPS, NSEQ), SEQ_MIN, SEQ_MAX + 1)
    counted = jax.random.randint(second, (GROUPS, 1), 2, NSEQ + 1)
    lengths = jnp.where(jnp.arange(NSEQ)[None, :] < counted, lengths, 0)
    fullest = jax.random.randint(third, (), 0, GROUPS)
    lengths = jnp.where(jnp.arange(GROUPS)[:, None] == fullest, SEQ_MAX, lengths)
    return lengths.astype(jnp.int32)


def steps_of(key, shape, cuts, least, top_value):
    def one(axis_at, parts):
        heights = jax.random.uniform(jax.random.fold_in(jax.random.fold_in(key, 6), axis_at), (parts,), jnp.float32, least / len(cuts), top_value / len(cuts))
        return jnp.repeat(jnp.exp(heights), shape[axis_at] // parts).reshape((-1,) + (1,) * (len(shape) - axis_at - 1))

    factor_of = one(*cuts[0])
    for cut in cuts[1:]:
        factor_of = factor_of * one(*cut)
    return factor_of


def bell_draw(stream_key, extent, scale, reach, cuts=(), held_as=jnp.bfloat16):
    loudness = steps_of(stream_key, extent, cuts, -0.22, 0.18) if cuts else 1.0
    values = jax.random.normal(stream_key, extent, jnp.float32) * scale * loudness
    return jnp.minimum(jnp.maximum(values, -reach), reach).astype(held_as)


def setup_inputs(seed: int = 0) -> dict:
    key_list = jax.random.split(jax.random.key(seed), 16)
    return {
        "tokens": bell_draw(key_list[0], (TOKENS, D), 1.0, 6.0, ((0, 32),)),
        "seq_lengths": draw_seq_lengths(jax.random.fold_in(key_list[15], 71), 0),
        "first_gain": jnp.clip(1.0 + 0.1 * jax.random.normal(key_list[2], (D,), jnp.float32), 0.5, 1.5),
        "mix_weight": bell_draw(key_list[3], (D, H * (2 * DK + 2 * DV)), D ** -0.5, 0.1875, ((1, 2),)),
        "rate_weight": bell_draw(key_list[4], (D, 2 * H), D ** -0.5, 0.1875, ((1, 2),)),
        "conv_weight": bell_draw(key_list[5], (CONV, H * (2 * DK + DV)), CONV ** -0.5, 3.0, ((1, 2),), jnp.float32),
        "decay_log": jnp.clip(-4.0 + 5.0 * jax.random.uniform(key_list[6], (H,), jnp.float32) ** steps_of(key_list[6], (H,), ((0, 2),), -0.2, 0.2), -4.0, 1.0),
        "decay_bias": jnp.clip(-4.0 + 5.0 * jax.random.uniform(key_list[7], (H,), jnp.float32) ** steps_of(key_list[7], (H,), ((0, 2),), -0.2, 0.2), -4.0, 1.0),
        "out_gain": jnp.clip(1.0 + 0.1 * jax.random.normal(key_list[8], (DV,), jnp.float32), 0.5, 1.5),
        "out_weight": bell_draw(key_list[9], (H * DV, D), DV ** -0.5, 0.375, ((0, 2),)),
        "second_gain": jnp.clip(1.0 + 0.1 * jax.random.normal(key_list[10], (D,), jnp.float32), 0.5, 1.5),
        "gate_weight": bell_draw(key_list[11], (D, FF), D ** -0.5, 0.1875, ((1, 2),)),
        "up_weight": bell_draw(key_list[12], (D, FF), D ** -0.5, 0.1875, ((1, 2),)),
        "down_weight": bell_draw(key_list[13], (FF, D), FF ** -0.5, 0.109375, ((0, 2),)),
        "cotangent": bell_draw(key_list[14], (TOKENS, D), 1.0, 6.0, ((0, 32),)),
    }


HIGH = lax.Precision.HIGHEST

@jax.custom_vjp
def low(v):
    return lax.optimization_barrier(v.astype(jnp.bfloat16)).astype(jnp.float32)

@jax.custom_vjp
def low_back(v):
    return v

def low_keep(v):
    return (low(v), None)

def low_pass(kept, grad):
    return (grad,)

def back_keep(v):
    return (v, None)

def back_low(kept, grad):
    return (low(grad),)
low.defvjp(low_keep, low_pass)
low_back.defvjp(back_keep, back_low)

def rms_norm(value, gain):
    return value * lax.rsqrt(lax.optimization_barrier(jnp.mean(value * value, axis=-1, keepdims=True)) + 1e-05) * gain

def layout(lengths, capacity):
    bounds = jnp.cumsum(lengths).astype(jnp.int32)
    position = jnp.arange(capacity, dtype=jnp.int32)
    segment = lax.optimization_barrier(jnp.sum((position[:, None] >= bounds[None, :]).astype(jnp.int32), axis=1)).astype(jnp.int32)
    live = (position < bounds[-1]).astype(jnp.float32)[:, None]
    return (segment, live)

def delta_head(query, keys, values, beta, decay, segment, span):
    total = query.shape[0]
    blocks = total // span
    q_block = query.reshape(blocks, span, -1)
    k_block = keys.reshape(blocks, span, -1)
    v_block = values.reshape(blocks, span, -1)
    b_block = beta.reshape(blocks, span)
    cumulative = jnp.cumsum(decay.reshape(blocks, span), axis=1)
    s_block = segment.reshape(blocks, span)
    before = jnp.concatenate([jnp.full((1,), -1, jnp.int32), s_block[:-1, -1]])
    carried = (s_block == before[:, None]).astype(jnp.float32)
    order = jnp.arange(span)
    within = (order[:, None] >= order[None, :])[None] & (s_block[:, :, None] == s_block[:, None, :])
    strict = within & (order[:, None] > order[None, :])[None]
    spread = jnp.where(within, cumulative[:, :, None] - cumulative[:, None, :], 0.0)
    fading = jnp.where(within, jnp.exp(spread), 0.0)
    inner = jnp.einsum('nid,njd->nij', k_block, k_block, precision=HIGH)
    lower = jnp.where(strict, b_block[:, :, None] * inner * fading, 0.0)
    system = jnp.eye(span, dtype=jnp.float32)[None] + lower
    start = jnp.exp(cumulative) * carried
    right = jnp.concatenate([b_block[:, :, None] * v_block, (b_block * start)[:, :, None] * k_block], axis=-1)
    solved = lax.linalg.triangular_solve(system, right, left_side=True, lower=True, unit_diagonal=True)
    width = v_block.shape[-1]
    u_part = solved[..., :width]
    w_part = solved[..., width:]
    scores = jnp.einsum('nid,njd->nij', q_block, k_block, precision=HIGH) * fading
    q_start = q_block * start[:, :, None]
    k_end = k_block * fading[:, -1, :, None]
    factor = start[:, -1]

    def step(state, pieces):
        w_now, u_now, k_now, q_now, s_now, f_now = pieces
        fresh = u_now - jnp.dot(w_now, state, precision=HIGH)
        out_now = jnp.dot(q_now, state, precision=HIGH) + jnp.dot(s_now, fresh, precision=HIGH)
        grown = f_now * state + lax.dot_general(k_now, fresh, (((0,), (0,)), ((), ())), precision=HIGH)
        return (grown, out_now)
    initial = jnp.zeros((k_block.shape[-1], width), jnp.float32)
    final, outputs = lax.scan(jax.checkpoint(step), initial, (w_part, u_part, k_end, q_start, scores, factor))
    return outputs.reshape(total, width)

def mixer(proj, rates, conv_w, decay_log, decay_bias, out_gain, segment, span):
    total = proj.shape[0]
    heads = decay_log.shape[0]
    lanes = 2 * DK + DV
    pieces = proj.reshape(total, heads, lanes + DV)
    blended = pieces[..., :lanes]
    gate_out = pieces[..., lanes:]
    taps = conv_w.reshape(CONV, heads, lanes)
    summed = jnp.zeros_like(blended)
    for back in range(CONV):
        moved = jnp.pad(blended, ((back, 0), (0, 0), (0, 0)))[:total]
        prior = jnp.pad(segment, (back, 0), constant_values=-1)[:total]
        summed = summed + jnp.where((prior == segment)[:, None, None], moved, 0.0) * taps[CONV - 1 - back]
    activated = jax.nn.silu(summed)
    query = activated[..., :DK]
    keys = activated[..., DK:2 * DK]
    values = activated[..., 2 * DK:]
    query = query * lax.rsqrt(lax.optimization_barrier(jnp.sum(query * query, axis=-1, keepdims=True)) + 1e-06) * DK ** (-0.5)
    keys = keys * lax.rsqrt(lax.optimization_barrier(jnp.sum(keys * keys, axis=-1, keepdims=True)) + 1e-06)
    halves = rates.reshape(total, heads, 2)
    beta = jax.nn.sigmoid(halves[..., 0])
    decay = -jnp.exp(decay_log) * jax.nn.softplus(halves[..., 1] + decay_bias)
    delta_out = jax.vmap(partial(delta_head, span=span), in_axes=(1, 1, 1, 1, 1, None), out_axes=1)(query, keys, values, beta, decay, segment)
    scaled = delta_out * lax.rsqrt(lax.optimization_barrier(jnp.mean(delta_out * delta_out, axis=-1, keepdims=True)) + 1e-05) * out_gain
    return (scaled * jax.nn.silu(gate_out)).reshape(total, heads * DV)

def matmul(left, right):
    return jnp.dot(left.astype(jnp.float32), right.astype(jnp.float32), precision=HIGH, preferred_element_type=jnp.float32)

def forward(params, inputs, segment, live):
    first_g, w_mix, w_rate, w_conv, d_log, d_bias, o_gain, w_out, second_g, w_gate, w_up, w_down = params
    first_normed = low(rms_norm(inputs, first_g))
    proj = low_back(matmul(first_normed, w_mix))
    rates = low_back(matmul(first_normed, w_rate))
    mixed = low(mixer(proj, rates, w_conv, d_log, d_bias, o_gain, segment, SPAN))
    attn = low_back(matmul(mixed, w_out))
    residual = inputs + live * attn
    second_normed = low(rms_norm(residual, second_g))
    gate = low_back(matmul(second_normed, w_gate))
    up = low_back(matmul(second_normed, w_up))
    hidden = low(jax.nn.silu(gate) * up)
    ffn = low_back(matmul(hidden, w_down))
    return residual + live * ffn

def reference(tokens, seq_lengths, first_gain, mix_weight, rate_weight, conv_weight, decay_log, decay_bias, out_gain, out_weight, second_gain, gate_weight, up_weight, down_weight, cotangent):
    params = (first_gain.astype(jnp.float32), mix_weight.astype(jnp.float32), rate_weight.astype(jnp.float32), conv_weight.astype(jnp.float32), decay_log.astype(jnp.float32), decay_bias.astype(jnp.float32), out_gain.astype(jnp.float32), out_weight.astype(jnp.float32), second_gain.astype(jnp.float32), gate_weight.astype(jnp.float32), up_weight.astype(jnp.float32), down_weight.astype(jnp.float32))
    groups = seq_lengths.shape[0]
    capacity = tokens.shape[0] // groups
    width = tokens.shape[1]
    inputs = tokens.astype(jnp.float32).reshape(groups, capacity, width)
    grads_in = cotangent.astype(jnp.float32).reshape(groups, capacity, width)

    def one_group(totals, item):
        group_x, group_cot, group_len = item
        segment, live = layout(group_len, capacity)
        result, backward = jax.vjp(lambda p, v: forward(p, v, segment, live), params, group_x)
        param_grads, input_grad = backward(group_cot)
        return (jax.tree.map(jnp.add, totals, param_grads), (result, input_grad))
    zeros = jax.tree.map(jnp.zeros_like, params)
    totals, (results, input_grads) = lax.scan(one_group, zeros, (inputs, grads_in, seq_lengths))
    return (results.reshape(groups * capacity, width).astype(jnp.bfloat16), input_grads.reshape(groups * capacity, width).astype(jnp.bfloat16), totals[0], totals[1], totals[2], totals[3], totals[4], totals[5], totals[6], totals[7], totals[8], totals[9], totals[10], totals[11])
```

```python
from functools import partial

import jax
import jax.numpy as jnp
from jax import lax
from jax.experimental import pallas as pl
from jax.experimental.pallas import tpu as pltpu
from jax.sharding import PartitionSpec as P

DK = 128
DV = 256
CONV = 4
CHUNK = 128
LANES = 2 * DK + DV
WIDE = LANES + DV
BASE = 8
PRIOR = 16
F32 = jnp.float32
LOW = jnp.bfloat16


def dot(a, b):
    return lax.dot_general(a, b, (((1,), (0,)), ((), ())), preferred_element_type=F32)


def dot_rows(a, b):
    return lax.dot_general(a, b, (((1,), (1,)), ((), ())), preferred_element_type=F32)


def dot_cols(a, b):
    return lax.dot_general(a, b, (((0,), (0,)), ((), ())), preferred_element_type=F32)


def halves(a):
    high = a.astype(LOW)
    return high, (a - high.astype(F32)).astype(LOW)


def unit_lower_inverse(lows):
    size = lows[0].shape[0]
    row = lax.broadcasted_iota(jnp.int32, (size, size), 0)
    col = lax.broadcasted_iota(jnp.int32, (size, size), 1)
    eye = (row == col).astype(F32)
    near = (row // BASE) == (col // BASE)
    first = [jnp.where(near, -a, 0.0) for a in lows]
    powers = [p.astype(LOW) for p in first]
    inverse = [eye + p for p in first]
    span = 2
    while span < BASE:
        powers = [dot(p, p).astype(LOW) for p in powers]
        inverse = [t + dot(p, t.astype(LOW)) for p, t in zip(powers, inverse)]
        span *= 2
    span = BASE
    while span < size:
        band = ((row // (2 * span)) == (col // (2 * span))) & ((row // span) > (col // span))
        held = [t.astype(LOW) for t in inverse]
        moved = [dot(jnp.where(band, a, 0.0).astype(LOW), t).astype(LOW) for a, t in zip(lows, held)]
        inverse = [t - dot(h, m) for t, h, m in zip(inverse, held, moved)]
        span *= 2
    parts = [halves(t) for t in inverse]
    news = []
    for a, t, (t_high, t_low) in zip(lows, inverse, parts):
        a_high, a_low = halves(a)
        left = eye - t - (dot(a_high, t_high) + (dot(a_high, t_low) + dot(a_low, t_high)))
        news.append(t + dot(t_high, left.astype(LOW)))
    return news


def masks(marks, line):
    size = marks.shape[0]
    row = lax.broadcasted_iota(jnp.int32, (size, size), 0)
    col = lax.broadcasted_iota(jnp.int32, (size, size), 1)
    same = marks[:, 6:7] == line[0:1, :]
    return (row >= col) & same, (row > col) & same


def col_of(vals, kind, head, heads):
    at = kind * heads + head
    return vals[:, at : at + 1]


def rate_terms(logits, params, marks, heads):
    size = logits.shape[0]
    row = lax.broadcasted_iota(jnp.int32, (size, size), 0)
    col = lax.broadcasted_iota(jnp.int32, (size, size), 1)
    until = (row >= col).astype(LOW)
    shifted = logits + params[0:1, :]
    soft = jnp.maximum(shifted, 0.0) + jnp.log1p(jnp.exp(-jnp.abs(shifted)))
    decay = params[1:2, :] * soft
    high, rest = halves(decay)
    middle, small = halves(decay - high.astype(F32))
    grown = dot(until, high) + (dot(until, middle) + dot(until, small))
    start = jnp.exp(grown) * marks[:, 7:8]
    last = jnp.exp(grown[size - 1 : size, :] - grown) * marks[:, 8:9]
    lane = lax.broadcasted_iota(jnp.int32, logits.shape, 1)
    packed = pltpu.roll(logits, 4 * heads, 1)
    packed = jnp.where(lane < 4 * heads, pltpu.roll(last, 2 * heads, 1), packed)
    packed = jnp.where(lane < 3 * heads, pltpu.roll(start, heads, 1), packed)
    packed = jnp.where(lane < 2 * heads, grown, packed)
    packed = jnp.where(lane < heads, sigmoid(logits), packed)
    return packed, grown.T[heads : 2 * heads]


def sigmoid(x):
    return 1.0 / (1.0 + jnp.exp(-x))


def conv_sum(ext, cols, taps, at):
    size = cols.shape[0]
    total = ext[PRIOR : PRIOR + size, at : at + LANES] * taps[CONV - 1 : CONV, at : at + LANES]
    for back in range(1, CONV):
        moved = ext[PRIOR - back : PRIOR - back + size, at : at + LANES]
        tap = taps[CONV - 1 - back : CONV - back, at : at + LANES]
        total = total + (cols[:, back - 1 : back] * moved) * tap
    return total


def fwd_kernel(pick_ref, own_ref, got_ref, marks_ref, line_ref, mix_ref, rate_ref, first_ref, params_ref, taps_ref,
               gain_ref, state_in, tail_in, *refs):
    (mixed_ref, first_out, proj_ref, vals_ref, rows_ref, s_ref, t_ref, f_ref, o_ref,
     state, tail, ext) = refs[-12:]
    heads = state.shape[0]
    size = CHUNK

    @pl.when(pl.program_id(0) == 0)
    def _():
        state[...] = state_in[...]
        tail[...] = tail_in[...]

    hs = range(heads)
    marks = marks_ref[...]
    pick = pick_ref[0, 0]
    x = pick * own_ref[...].astype(F32) + (1.0 - pick) * got_ref[...].astype(F32)
    first = x * lax.rsqrt(jnp.mean(x * x, axis=1, keepdims=True) + 1e-05) * first_ref[...]
    first = first.astype(LOW)
    first_out[...] = first
    vals, grown = rate_terms(dot(first, rate_ref[...]), params_ref[...], marks, heads)
    vals_ref[...] = vals
    rows_ref[0:heads, :] = grown
    within, strict = masks(marks, line_ref[...])
    ext[0:PRIOR, :] = tail[...]
    for h in hs:
        at = h * LANES
        proj = dot(first, mix_ref[:, h * WIDE : (h + 1) * WIDE])
        proj_ref[:, h * WIDE : (h + 1) * WIDE] = proj
        ext[PRIOR : PRIOR + size, at : at + LANES] = proj[:, :LANES]
        tail[:, at : at + LANES] = proj[size - PRIOR :, :LANES]
    qs, ks, vs, betas, starts, lasts, fades = [], [], [], [], [], [], []
    for h in hs:
        summed = conv_sum(ext, marks, taps_ref, h * LANES)
        act = summed * sigmoid(summed)
        q = act[:, :DK]
        k = act[:, DK : 2 * DK]
        qs.append(q * (lax.rsqrt(jnp.sum(q * q, axis=1, keepdims=True) + 1e-06) * DK ** (-0.5)))
        ks.append(k * lax.rsqrt(jnp.sum(k * k, axis=1, keepdims=True) + 1e-06))
        vs.append(act[:, 2 * DK :])
        betas.append(col_of(vals, 0, h, heads))
        starts.append(col_of(vals, 2, h, heads))
        lasts.append(col_of(vals, 3, h, heads))
        spread = col_of(vals, 1, h, heads) - grown[h : h + 1, :]
        fades.append(jnp.exp(jnp.where(within, spread, -1e9)))
    stacks = [jnp.concatenate([q, k], axis=0).astype(LOW) for q, k in zip(qs, ks)]
    klows = [s[size:] for s in stacks]
    inner = [dot_rows(s, k) for s, k in zip(stacks, klows)]
    scores = [(i[:size] * m).astype(LOW) for i, m in zip(inner, fades)]
    lows = [jnp.where(strict, b * (i[size:] * m), 0.0) for b, i, m in zip(betas, inner, fades)]
    solve = [t.astype(LOW) for t in unit_lower_inverse(lows)]
    olds = [state[h] for h in hs]
    held = [s.astype(LOW) for s in olds]
    reads = [dot(q, s) for q, s in zip(stacks, held)]
    right = [(b * (v - e * r[size:])).astype(LOW) for b, v, e, r in zip(betas, vs, starts, reads)]
    fresh = [dot(t, x).astype(LOW) for t, x in zip(solve, right)]
    ends = [(l * k).astype(LOW) for l, k in zip(lasts, ks)]
    grows = [dot_cols(k, f) for k, f in zip(ends, fresh)]
    for h in hs:
        state[h] = starts[h][size - 1 : size, :] * olds[h] + grows[h]
    outs = [e * r[:size] + dot(p, f) for e, r, p, f in zip(starts, reads, scores, fresh)]
    gain = gain_ref[...]
    for h in hs:
        o = outs[h]
        gate = proj_ref[:, h * WIDE + LANES : (h + 1) * WIDE]
        scaled = o * lax.rsqrt(jnp.mean(o * o, axis=1, keepdims=True) + 1e-05) * gain
        mixed_ref[:, h * DV : (h + 1) * DV] = (scaled * (gate * sigmoid(gate))).astype(LOW)
        s_ref[0, h] = held[h]
        t_ref[0, h] = solve[h]
        f_ref[:, h * DV : (h + 1) * DV] = fresh[h]
        o_ref[:, h * DV : (h + 1) * DV] = o.astype(LOW)


def fold(x):
    return jnp.sum(x.reshape(x.shape[0] // 8, 8, x.shape[1]), axis=0)


def bwd_kernel(dmix_ref, prev_ref, proj_ref, marks_ref, line_ref, vals_ref, rows_ref, taps_ref, gain_ref,
               s_ref, t_ref, f_ref, o_ref,
               dproj_ref, dcols_ref, drows_ref, dtaps_ref, dgain_ref, dstate, ext, after,
               *, first, total_heads):
    heads = dstate.shape[0]
    size = CHUNK

    @pl.when(pl.program_id(0) == 0)
    def _():
        dstate[...] = jnp.zeros_like(dstate)
        after[...] = jnp.zeros_like(after)
        dtaps_ref[...] = jnp.zeros_like(dtaps_ref)
        dgain_ref[...] = jnp.zeros_like(dgain_ref)

    marks = marks_ref[...]
    vals = vals_ref[...]
    rows = rows_ref[...]
    within, strict = masks(marks, line_ref[...])
    gain = gain_ref[...]
    for h in range(heads):
        at = h * LANES
        ext[0:PRIOR, at : at + LANES] = prev_ref[:, h * WIDE : h * WIDE + LANES].astype(F32)
        ext[PRIOR : PRIOR + size, at : at + LANES] = proj_ref[:, h * WIDE : h * WIDE + LANES].astype(F32)
    hs = range(heads)
    summed = [conv_sum(ext, marks, taps_ref, h * LANES) for h in hs]
    sig = [sigmoid(s) for s in summed]
    act = [s * g for s, g in zip(summed, sig)]
    slope = [g * (1.0 + s * (1.0 - g)) for s, g in zip(summed, sig)]
    rq = [lax.rsqrt(jnp.sum(a[:, :DK] * a[:, :DK], axis=1, keepdims=True) + 1e-06) for a in act]
    rk = [lax.rsqrt(jnp.sum(a[:, DK : 2 * DK] * a[:, DK : 2 * DK], axis=1, keepdims=True) + 1e-06) for a in act]
    qn = [a[:, :DK] * r for a, r in zip(act, rq)]
    ks = [a[:, DK : 2 * DK] * r for a, r in zip(act, rk)]
    vs = [a[:, 2 * DK :] for a in act]
    betas = [col_of(vals, 0, first + h, total_heads) for h in hs]
    starts = [col_of(vals, 2, first + h, total_heads) for h in hs]
    lasts = [col_of(vals, 3, first + h, total_heads) for h in hs]
    fades = [
        jnp.exp(jnp.where(within, col_of(vals, 1, first + h, total_heads) - rows[first + h : first + h + 1, :], -1e9)) for h in hs
    ]
    stacks = [jnp.concatenate([q * DK ** (-0.5), k], axis=0).astype(LOW) for q, k in zip(qn, ks)]
    qlows = [s[:size] for s in stacks]
    klows = [s[size:] for s in stacks]
    inner = [dot_rows(s, k) for s, k in zip(stacks, klows)]
    scores = [i[:size] * m for i, m in zip(inner, fades)]
    pairs = [jnp.where(strict, i[size:] * m, 0.0) for i, m in zip(inner, fades)]
    held = [s_ref[0, h] for h in hs]
    reads = [dot(q, s) for q, s in zip(stacks, held)]
    douts = []
    for h in hs:
        o = o_ref[:, h * DV : (h + 1) * DV].astype(F32)
        gate = proj_ref[:, h * WIDE + LANES : (h + 1) * WIDE].astype(F32)
        dmix = dmix_ref[:, h * DV : (h + 1) * DV].astype(F32)
        r = lax.rsqrt(jnp.mean(o * o, axis=1, keepdims=True) + 1e-05)
        g = sigmoid(gate)
        on = o * r
        u = dmix * (gate * g)
        dgain_ref[...] += fold(u * on)
        dgate = (dmix * on * gain) * (g * (1.0 + gate * (1.0 - g)))
        dproj_ref[:, h * WIDE + LANES : (h + 1) * WIDE] = dgate.astype(LOW)
        w = u * gain
        douts.append(r * (w - on * jnp.mean(w * on, axis=1, keepdims=True)))
    dlows = [d.astype(LOW) for d in douts]
    dnexts = [dstate[h] for h in hs]
    dheld = [d.astype(LOW) for d in dnexts]
    ends = [(l * k).astype(LOW) for l, k in zip(lasts, ks)]
    solve = [t_ref[0, h] for h in hs]
    fresh = [f_ref[:, h * DV : (h + 1) * DV] for h in hs]
    dfresh = [dot_cols(p.astype(LOW), d) + dot(k, s) for p, d, k, s in zip(scores, dlows, ends, dheld)]
    dright = [dot_cols(t, d.astype(LOW)) for t, d in zip(solve, dfresh)]
    outer = [
        dot_rows(jnp.concatenate([d, x.astype(LOW)], axis=0), f)
        for d, x, f in zip(dlows, dright, fresh)
    ]
    scaled = [b * x for b, x in zip(betas, dright)]
    dreads = [
        jnp.concatenate([e * d, -e * x], axis=0).astype(LOW) for e, d, x in zip(starts, douts, scaled)
    ]
    for h in hs:
        dstate[h] = starts[h][size - 1 : size, :] * dnexts[h] + dot_cols(stacks[h], dreads[h])
    dqk = [dot_rows(d, s) for d, s in zip(dreads, held)]
    dend = [dot_rows(f, s) for f, s in zip(fresh, dheld)]
    last_row = lax.broadcasted_iota(jnp.int32, (size, 1), 0) == size - 1
    dscore = [o[:size] * m for o, m in zip(outer, fades)]
    dpair = [-o[size:] for o in outer]
    dinner = [jnp.where(strict, b * d * m, 0.0) for b, d, m in zip(betas, dpair, fades)]
    dq_in = [dot(d.astype(LOW), k) for d, k in zip(dscore, klows)]
    dk_in = [
        dot_cols(d.astype(LOW), q) + dot((i + i.T).astype(LOW), k)
        for d, q, i, k in zip(dscore, qlows, dinner, klows)
    ]
    for h in hs:
        e, b, dr, y, z = starts[h], betas[h], dright[h], reads[h][:size], reads[h][size:]
        weights = scores[h] * outer[h][:size] + b * pairs[h] * dpair[h]
        dbeta = jnp.sum(dr * (vs[h] - e * z), axis=1, keepdims=True) + jnp.sum(
            dpair[h] * pairs[h], axis=1, keepdims=True
        )
        dstart = jnp.sum(douts[h] * y - scaled[h] * z, axis=1, keepdims=True)
        through = jnp.sum(dnexts[h] * held[h].astype(F32))
        dstart = dstart + jnp.where(last_row, through, 0.0)
        dlast = jnp.sum(ks[h] * dend[h], axis=1, keepdims=True)
        at = h
        dcols_ref[:, at : at + 1] = dbeta
        dcols_ref[:, heads + at : heads + at + 1] = jnp.sum(weights, axis=1, keepdims=True)
        dcols_ref[:, 2 * heads + at : 2 * heads + at + 1] = dstart
        dcols_ref[:, 3 * heads + at : 3 * heads + at + 1] = dlast
        drows_ref[h : h + 1, :] = jnp.sum(weights, axis=0, keepdims=True)
    for h in hs:
        dq = dqk[h][:size] + dq_in[h]
        dk = dqk[h][size:] + dk_in[h] + lasts[h] * dend[h]
        dv = scaled[h]
        dq = (rq[h] * DK ** (-0.5)) * (dq - qn[h] * jnp.sum(dq * qn[h], axis=1, keepdims=True))
        dk = rk[h] * (dk - ks[h] * jnp.sum(dk * ks[h], axis=1, keepdims=True))
        at = h * LANES
        dsum = jnp.concatenate([dq, dk, dv], axis=1) * slope[h]
        after[0:size, at : at + LANES] = dsum
        here = slice(at, at + LANES)
        dproj = dsum * taps_ref[CONV - 1 : CONV, here]
        dtaps_ref[CONV - 1, :, here] += fold(dsum * ext[PRIOR : PRIOR + size, here])
        for back in range(1, CONV):
            moved = ext[PRIOR - back : PRIOR - back + size, here]
            dtaps_ref[CONV - 1 - back, :, here] += fold((marks[:, back - 1 : back] * moved) * dsum)
            later = after[back : back + size, here]
            dproj = dproj + (marks[:, 2 + back : 3 + back] * later) * taps_ref[CONV - 1 - back : CONV - back, here]
        dproj_ref[:, h * WIDE : h * WIDE + LANES] = dproj.astype(LOW)
        after[size : size + 8, here] = dsum[0:8]


PARAMS = pltpu.CompilerParams(
    dimension_semantics=("arbitrary",), vmem_limit_bytes=56 * 1024 * 1024
)


def fixed(shape):
    return pl.BlockSpec(shape, lambda i: (0,) * len(shape), pipeline_mode=pl.Buffered(1))


def cost(total, heads):
    return pl.CostEstimate(
        flops=10_000_000 * total * heads, bytes_accessed=total * heads * 8192, transcendentals=0
    )


def mixer_fwd(pick, x, got, marks, line, weights, state, tail, kept, at):
    mix_w, rate_w, first_gain, params, taps, gain = weights
    total, width = line.shape[1], x.shape[1]
    heads = mix_w.shape[1] // WIDE
    chunks = total // CHUNK
    rows_at = lambda i: (at + i, 0)
    blocks_at = lambda i: (at + i, 0, 0, 0)
    whole = [
        (pl.BlockSpec((CHUNK, width), rows_at), (total, width), LOW),
        (pl.BlockSpec((CHUNK, heads * WIDE), rows_at), (total, heads * WIDE), F32),
        (pl.BlockSpec((CHUNK, 128), rows_at), (total, 128), F32),
        (pl.BlockSpec((8, CHUNK), lambda i: (0, at + i)), (8, total), F32),
        (pl.BlockSpec((1, heads, DK, DV), blocks_at), (chunks, heads, DK, DV), LOW),
        (pl.BlockSpec((1, heads, CHUNK, CHUNK), blocks_at), (chunks, heads, CHUNK, CHUNK), LOW),
        (pl.BlockSpec((CHUNK, heads * DV), rows_at), (total, heads * DV), LOW),
        (pl.BlockSpec((CHUNK, heads * DV), rows_at), (total, heads * DV), LOW),
    ]
    in_specs = [
        pl.BlockSpec(memory_space=pltpu.SMEM),
        pl.BlockSpec((CHUNK, width), lambda i: (i, 0)),
        pl.BlockSpec((CHUNK, width), lambda i: (i, 0)),
        pl.BlockSpec((CHUNK, marks.shape[1]), rows_at),
        pl.BlockSpec((8, CHUNK), lambda i: (0, at + i)),
        fixed(mix_w.shape),
        fixed(rate_w.shape),
        fixed(first_gain.shape),
        fixed(params.shape),
        fixed(taps.shape),
        fixed(gain.shape),
        fixed((heads, DK, DV)),
        fixed((PRIOR, heads * LANES)),
    ]
    out = pl.pallas_call(
        fwd_kernel,
        grid=(x.shape[0] // CHUNK,),
        in_specs=in_specs + [pl.BlockSpec(memory_space=pl.ANY)] * len(kept),
        out_specs=[pl.BlockSpec((CHUNK, heads * DV), lambda i: (i, 0))]
        + [w[0] for w in whole]
        + [
            pl.BlockSpec((heads, DK, DV), lambda i: (0, 0, 0)),
            pl.BlockSpec((PRIOR, heads * LANES), lambda i: (0, 0)),
        ],
        out_shape=[jax.ShapeDtypeStruct((x.shape[0], heads * DV), LOW)]
        + [jax.ShapeDtypeStruct(w[1], w[2]) for w in whole]
        + [
            jax.ShapeDtypeStruct((heads, DK, DV), F32),
            jax.ShapeDtypeStruct((PRIOR, heads * LANES), F32),
        ],
        scratch_shapes=[pltpu.VMEM((CHUNK + PRIOR, heads * LANES), F32)],
        input_output_aliases={len(in_specs) + n: 1 + n for n in range(len(kept))},
        compiler_params=PARAMS,
        cost_estimate=cost(x.shape[0], heads),
        name="mixer_forward",
    )(pick, x, got, marks, line, mix_w, rate_w, first_gain, params, taps, gain, state, tail, *kept)
    return out[0], out[1:9], out[9], out[10]


def mixer_bwd(dmixed, marks, line, taps, gain, kept, group, groups):
    proj, vals, rows, states, solves, fresh, outs = kept
    total = proj.shape[0]
    whole = proj.shape[1] // WIDE
    heads = whole // groups
    chunks = total // CHUNK
    per = CHUNK // PRIOR
    at = lambda i: chunks - 1 - i
    return pl.pallas_call(
        partial(bwd_kernel, first=group * heads, total_heads=whole),
        grid=(chunks,),
        in_specs=[
            pl.BlockSpec((CHUNK, heads * DV), lambda i: (at(i), group)),
            pl.BlockSpec((PRIOR, heads * WIDE), lambda i: (jnp.maximum(at(i) * per - 1, 0), group)),
            pl.BlockSpec((CHUNK, heads * WIDE), lambda i: (at(i), group)),
            pl.BlockSpec((CHUNK, marks.shape[1]), lambda i: (at(i), 0)),
            pl.BlockSpec((8, CHUNK), lambda i: (0, at(i))),
            pl.BlockSpec((CHUNK, 128), lambda i: (at(i), 0)),
            pl.BlockSpec((rows.shape[0], CHUNK), lambda i: (0, at(i))),
            pl.BlockSpec((CONV, heads * LANES), lambda i: (0, group)),
            pl.BlockSpec((1, DV), lambda i: (0, 0)),
            pl.BlockSpec((1, heads, DK, DV), lambda i: (at(i), group, 0, 0)),
            pl.BlockSpec((1, heads, CHUNK, CHUNK), lambda i: (at(i), group, 0, 0)),
            pl.BlockSpec((CHUNK, heads * DV), lambda i: (at(i), group)),
            pl.BlockSpec((CHUNK, heads * DV), lambda i: (at(i), group)),
        ],
        out_specs=[
            pl.BlockSpec((CHUNK, heads * WIDE), lambda i: (at(i), 0)),
            pl.BlockSpec((CHUNK, 4 * heads), lambda i: (at(i), 0)),
            pl.BlockSpec((8, CHUNK), lambda i: (0, at(i))),
            pl.BlockSpec((CONV, 8, heads * LANES), lambda i: (0, 0, 0)),
            pl.BlockSpec((8, DV), lambda i: (0, 0)),
        ],
        out_shape=[
            jax.ShapeDtypeStruct((total, heads * WIDE), LOW),
            jax.ShapeDtypeStruct((total, 4 * heads), F32),
            jax.ShapeDtypeStruct((8, total), F32),
            jax.ShapeDtypeStruct((CONV, 8, heads * LANES), F32),
            jax.ShapeDtypeStruct((8, DV), F32),
        ],
        scratch_shapes=[
            pltpu.VMEM((heads, DK, DV), F32),
            pltpu.VMEM((CHUNK + PRIOR, heads * LANES), F32),
            pltpu.VMEM((CHUNK + 8, heads * LANES), F32),
        ],
        compiler_params=PARAMS,
        cost_estimate=cost(total, heads),
        name="mixer_backward",
    )(dmixed, proj, proj, marks, line, vals, rows, taps, gain, states, solves, fresh, outs)


def merge_back(parts, heads):
    each = heads // len(parts)
    cut = [[p[1][:, k * each : (k + 1) * each] for p in parts] for k in range(4)]
    dbeta, dgrown, dstart, dlast = [jnp.concatenate(c, axis=1) for c in cut]
    dgrown = dgrown - jnp.concatenate([p[2][:each] for p in parts], axis=0).T
    dtaps = jnp.concatenate([jnp.sum(p[3], axis=1) for p in parts], axis=1)
    dgain = sum(jnp.sum(p[4], axis=0) for p in parts)
    return (dbeta, dgrown, dstart, dlast), dtaps, dgain


def prep(rates, decay_log, decay_bias, segment):
    total = rates.shape[0]
    heads = decay_log.shape[0]
    chunks = total // CHUNK
    pieces = rates.reshape(total, heads, 2)
    beta = jax.nn.sigmoid(pieces[..., 0])
    decay = -jnp.exp(decay_log) * jax.nn.softplus(pieces[..., 1] + decay_bias)
    order = jnp.arange(CHUNK)
    until = (order[:, None] >= order[None, :]).astype(F32)
    grown = jnp.einsum(
        "ij,njh->nih", until, decay.reshape(chunks, CHUNK, heads), precision=lax.Precision.HIGHEST
    )
    seg = segment.reshape(chunks, CHUNK)
    before = jnp.concatenate([jnp.full((1,), -1, jnp.int32), seg[:-1, -1]])
    carried = (seg == before[:, None])[:, :, None]
    start = jnp.where(carried, jnp.exp(grown), 0.0)
    ending = (seg == seg[:, -1:])[:, :, None]
    last = jnp.where(ending, jnp.exp(jnp.where(ending, grown[:, -1:] - grown, 0.0)), 0.0)
    return (
        beta,
        grown.reshape(total, heads),
        start.reshape(total, heads),
        last.reshape(total, heads),
    )


def tables(segment):
    total = segment.shape[0]
    seg = segment.reshape(-1, CHUNK)
    before = jnp.concatenate([jnp.full((1,), -1, jnp.int32), seg[:-1, -1]])
    marks = []
    for back in range(1, CONV):
        prior = jnp.pad(segment, (back, 0), constant_values=-1)[:total]
        marks.append(prior == segment)
    for back in range(1, CONV):
        later = jnp.pad(segment, (0, back), constant_values=-1)[back:]
        marks.append(later == segment)
    marks.append(segment)
    marks.append((seg == before[:, None]).reshape(total))
    marks.append((seg == seg[:, -1:]).reshape(total))
    marks += [jnp.zeros((total,), F32)] * 7
    marks = jnp.stack([m.astype(F32) for m in marks], axis=1)
    return marks, jnp.broadcast_to(segment.astype(F32)[None], (8, total))


def mixer_weights(mix_w, rate_w, first_gain, decay_log, decay_bias, taps, gain):
    heads = decay_log.shape[0]
    paired_w = rate_w.reshape(-1, heads, 2)
    filled = jnp.concatenate([paired_w[..., 0], paired_w[..., 1]], axis=1)
    filled = jnp.pad(filled, ((0, 0), (0, 128 - 2 * heads)))
    params = jnp.zeros((8, 128), F32)
    params = params.at[0, heads : 2 * heads].set(decay_bias)
    params = params.at[1, heads : 2 * heads].set(-jnp.exp(decay_log))
    return mix_w, filled, first_gain[None], params, taps, gain[None]


def rates_back(vals, decay_log, decay_bias, segment, grads):
    heads = decay_log.shape[0]
    logits = vals[:, 4 * heads : 6 * heads].reshape(-1, 2, heads).transpose(0, 2, 1)
    rates = logits.reshape(-1, 2 * heads)
    back = jax.vjp(lambda r, l, b: prep(r, l, b, segment), rates, decay_log, decay_bias)[1]
    return back(grads)


def cross(left, right):
    return lax.dot_general(
        left, right, (((0,), (0,)), ((), ())), preferred_element_type=F32
    )


def wide_dot(left, right):
    return jnp.dot(left, right, preferred_element_type=F32)


def back_dot(grad, weight):
    return lax.dot_general(
        grad, weight, (((1,), (1,)), ((), ())), preferred_element_type=F32
    )


def norm_parts(value):
    return lax.rsqrt(jnp.mean(value * value, axis=-1, keepdims=True) + 1e-05)


def norm_back(value, scale, gain, grad):
    u = gain * grad
    part = scale * u - value * (scale * scale * scale) * jnp.mean(u * value, axis=-1, keepdims=True)
    return part, jnp.sum(grad * value * scale, axis=0)


def layout(lengths, capacity):
    bounds = jnp.cumsum(lengths)
    position = jnp.arange(capacity, dtype=jnp.int32)
    segment = jnp.sum((position[:, None] >= bounds[None, :]).astype(jnp.int32), axis=1)
    live = (position < bounds[-1]).astype(F32)[:, None]
    return segment, live


class Pair:
    def __init__(self, groups):
        self.here = lax.axis_index("tensor")
        self.core = lax.axis_index("dp") % 2
        self.side = (lax.axis_index("dp") // 2) % 2
        self.cores = [(i, i ^ 1) for i in range(groups)]
        self.sides = [(i, i ^ 2) for i in range(groups)]
        self.groups = groups

    def across(self, value):
        return lax.ppermute(value, "tensor", [(0, 1), (1, 0)])

    def beside(self, value):
        return lax.ppermute(value, "dp", self.cores)

    def along(self, value):
        return lax.ppermute(value, "dp", self.sides)

    def part(self, value, which):
        size = value.shape[0] // 2
        return lax.dynamic_slice_in_dim(value, which * size, size, 0)

    def join(self, mine, other, which):
        low = jnp.where(which == 0, mine, other)
        return jnp.concatenate([low, jnp.where(which == 0, other, mine)], axis=0)

    def halve(self, value):
        mine = self.part(value, self.core).astype(F32)
        got = self.beside(self.part(value, 1 - self.core)).astype(F32)
        return (mine + got).astype(LOW)

    def quarter(self, half):
        mine = self.part(half, self.side).astype(F32)
        got = self.along(self.part(half, 1 - self.side)).astype(F32)
        return (mine + got).astype(LOW)

    def sum(self, values, turn, alike=2):
        orders = []
        for c in range(alike):
            order = list(range(c, self.groups, alike))
            order = order[turn:] + order[:turn]
            orders.append(order)
        return lax.psum(values, "dp", axis_index_groups=orders)

    def halves(self, values):
        return [self.join(v, self.along(v), self.side) for v in values]

    def everywhere(self, value):
        step = 1
        while step < self.groups:
            value = value + lax.ppermute(value, "dp", [(i, i ^ step) for i in range(self.groups)])
            step *= 2
        return value

    def whole(self, values):
        return [self.join(v, self.beside(v), self.core).astype(F32) for v in values]


def feed_forward(residual, live, second_gain, gate_w, up_w, down_w, out_grad):
    scale = norm_parts(residual)
    second_low = (residual * scale * second_gain).astype(LOW)
    gate = wide_dot(second_low, gate_w)
    up = wide_dot(second_low, up_w)
    sigma = jax.nn.sigmoid(gate)
    gated = gate * sigma
    hidden = (gated * up).astype(LOW)
    block_out = (residual + live * wide_dot(hidden, down_w)).astype(LOW)
    ffn_grad = (live * out_grad).astype(LOW)
    hidden_grad = back_dot(ffn_grad, down_w)
    gate_grad = (hidden_grad * up * (sigma * (1.0 + gate * (1.0 - sigma)))).astype(LOW)
    up_grad = (hidden_grad * gated).astype(LOW)
    second_sum = back_dot(gate_grad, gate_w) + back_dot(up_grad, up_w)
    part, gain_part = norm_back(residual, scale, second_gain, second_sum)
    residual_grad = out_grad + part
    pieces = (second_low, hidden, ffn_grad, gate_grad, up_grad)
    return block_out, residual_grad, gain_part, pieces


def tied(*values):
    return lax.optimization_barrier(values)


def paired(
    tokens, seq_lengths, first_gain, mix_weight, rate_weight, conv_weight, decay_log, decay_bias,
    out_gain, out_weight, second_gain, gate_weight, up_weight, down_weight, cotangent,
):
    rows = tokens.shape[0]
    capacity = rows * 2
    move = Pair(lax.axis_size("dp"))
    here = move.here
    heads = decay_log.shape[0]
    cuts = 3 if rows % (3 * CHUNK) == 0 else 1
    piece = rows // cuts
    own = [tokens[j * piece : (j + 1) * piece] for j in range(cuts)]
    got = [move.across(own[0])]
    for j in range(1, cuts):
        got[-1], own[j] = tied(got[-1], own[j])
        got.append(move.across(own[j]))
    gate_src, up_src, down_src, last_got = tied(gate_weight, up_weight, down_weight, got[-1])
    got[-1] = last_got
    fetched = [
        move.across(move.part(move.part(w, move.core), move.side))
        for w in (gate_src, up_src, down_src)
    ]
    segment, live_all = layout(seq_lengths[0], capacity)
    live = lax.dynamic_slice_in_dim(live_all, here * rows, rows, 0)
    marks, line = tables(segment)
    weights = mixer_weights(
        mix_weight, rate_weight, first_gain, decay_log, decay_bias, conv_weight, out_gain
    )
    state = jnp.zeros((heads, DK, DV), F32)
    tail = jnp.zeros((PRIOR, heads * LANES), F32)
    first_half = (here == 0).astype(F32).reshape(1, 1)
    per = piece // CHUNK
    mixed, kept, attn_own, attn_got = [], (), [], []
    for p in range(2 * cuts):
        pick = first_half if p < cuts else 1.0 - first_half
        now, kept, state, tail = mixer_fwd(pick, own[p % cuts], got[p % cuts], marks, line, weights, state, tail, kept, p * per)
        mixed.append(now)
        if p == cuts:
            fetched, state = tied(fetched, state)
            fetched = [move.join(f, move.along(f), move.side) for f in fetched]
        if p >= cuts:
            low, high = wide_dot(mixed[p - cuts], out_weight), wide_dot(now, out_weight)
            attn_own.append(jnp.where(here == 0, low, high))
            attn_got.append(move.across(jnp.where(here == 0, high, low).astype(LOW)))
    fetched, mixed[-1] = tied(fetched, mixed[-1])
    others = [move.join(f, move.beside(f), move.core) for f in fetched]
    gate_w = jnp.concatenate([gate_weight, others[0]], axis=1)
    up_w = jnp.concatenate([up_weight, others[1]], axis=1)
    down_w = jnp.concatenate([down_weight, others[2]], axis=0)
    attn_got, gate_w, up_w, down_w = tied(attn_got, gate_w, up_w, down_w)
    attn = jnp.concatenate([a + g.astype(F32) for a, g in zip(attn_own, attn_got)], axis=0)
    first_rows, kept = kept[0], kept[1:]
    inputs = tokens.astype(F32)
    residual = inputs + live * attn

    width = gate_weight.shape[1]
    out_grad = cotangent.astype(F32)
    scale = norm_parts(residual)
    second_low = (residual * scale * second_gain).astype(LOW)
    gate = wide_dot(second_low, gate_w)
    up = wide_dot(second_low, up_w)
    sigma = jax.nn.sigmoid(gate)
    gated = gate * sigma
    hidden = (gated * up).astype(LOW)
    ffn_grad = (live * out_grad).astype(LOW)
    hidden_grad = back_dot(ffn_grad, down_w)
    gate_grad = (hidden_grad * up * (sigma * (1.0 + gate * (1.0 - sigma)))).astype(LOW)
    up_grad = (hidden_grad * gated).astype(LOW)
    grad_down = cross(hidden, ffn_grad).astype(LOW)
    down_halves = [move.halve(grad_down[:width]), move.halve(grad_down[width:])]
    gate_half = move.halve(cross(second_low, gate_grad).astype(LOW))
    up_half = move.halve(cross(second_low, up_grad).astype(LOW))
    down_mine, down_sent = [move.quarter(d) for d in down_halves]
    gate_in, up_in, down_mine, down_sent, gate_half, up_half = tied(
        gate_grad, up_grad, down_mine, down_sent, gate_half, up_half
    )
    gate_half, up_half = move.quarter(gate_half), move.quarter(up_half)
    down_sent = move.across(down_sent)
    gate_sent = move.across(gate_half[:, width:])
    up_sent = move.across(up_half[:, width:])
    second_sum = back_dot(gate_in, gate_w) + back_dot(up_in, up_w)
    part, second_part = norm_back(residual, scale, second_gain, second_sum)
    residual_grad = out_grad + part
    attn_low = (live * residual_grad).astype(LOW)
    attn_sent = move.across(attn_low)
    attn_low, hidden_in = tied(attn_low, hidden)
    block_out = (residual + live * wide_dot(hidden_in, down_w)).astype(LOW)
    mixed = jnp.concatenate(mixed, axis=0)
    gate_sum = gate_half[:, :width] + gate_sent
    up_sum = up_half[:, :width] + up_sent
    attn_sent, block_out, mixed, gate_sum, up_sum, down_sum = tied(
        attn_sent, block_out, mixed, gate_sum, up_sum, down_mine + down_sent
    )
    attn_grad = move.join(attn_low, attn_sent, here)
    dmixed = back_dot(attn_grad, out_weight).astype(LOW)
    grad_out = move.quarter(move.halve(cross(mixed, attn_grad).astype(LOW)))

    dmixed, sums_ffn_in = tied(dmixed, (gate_sum, up_sum, down_sum, grad_out))
    sums_ffn = move.sum(sums_ffn_in, 0, 4)
    back = mixer_bwd(dmixed, marks, line, conv_weight, out_gain[None], kept, 0, 1)
    back, sums_ffn = tied(back, sums_ffn)
    dproj = back[0]
    sums_ffn = move.halves(sums_ffn)
    dprep, dtaps, dgain = merge_back([back], heads)
    rates_grad, grad_log, grad_bias = rates_back(
        kept[1], decay_log, decay_bias, segment, dprep
    )
    rates_low = rates_grad.astype(LOW)

    def first_part(dproj, which):
        return back_dot(move.part(rates_low, which), rate_weight) + back_dot(
            move.part(dproj, which), mix_weight
        )

    theirs = first_part(dproj, 1 - here)
    theirs_low = theirs.astype(LOW)
    dproj, theirs_low = tied(dproj, theirs_low)
    sent = move.across(theirs_low)
    half = move.halve(cross(first_rows, dproj).astype(LOW))
    dproj, half, sums_ffn = tied(dproj, half, sums_ffn)
    (sum_mix,) = move.sum((half,), 1)
    mine = first_part(dproj, here)
    grad_rate = cross(rates_low, first_rows)
    token_own = inputs
    token_other = jnp.concatenate(got, axis=0).astype(F32)
    first_scale = norm_parts(token_own)
    first_part_gain = jnp.sum(mine * token_own * first_scale, axis=0) + jnp.sum(
        theirs * token_other * norm_parts(token_other), axis=0
    )
    model = first_gain.shape[0]
    thin = jnp.concatenate([dgain, grad_log, grad_bias])
    thin = jnp.pad(thin, (0, model - thin.shape[0]))
    small = jnp.concatenate(
        [first_part_gain[None], second_part[None], thin[None], grad_rate, dtaps.reshape(-1, model)]
    )
    small = move.everywhere(small)
    gains = small[:3] + move.across(small[:3])
    grad_first, grad_second, grad_outg = gains[0], gains[1], gains[2, :DV]
    grad_log = small[2, DV : DV + heads]
    grad_bias = small[2, DV + heads : DV + 2 * heads]
    grad_rate = small[3 : 3 + 2 * heads].T
    grad_conv = small[3 + 2 * heads :].reshape(dtaps.shape)

    grad_gate, grad_up, grad_down, grad_out = move.whole(sums_ffn)
    sent, grad_gate, grad_up, grad_down, grad_out = tied(
        sent, grad_gate, grad_up, grad_down, grad_out
    )
    input_part, _ = norm_back(inputs, first_scale, first_gain, mine + sent.astype(F32))
    tokens_grad = (residual_grad + input_part).astype(LOW)
    early = (
        block_out, tokens_grad, grad_first, grad_rate, grad_conv, grad_log, grad_bias,
        grad_outg, grad_second, grad_gate, grad_up, grad_down, grad_out,
    )
    early, sum_mix = tied(early, sum_mix)
    (grad_mix,) = move.whole((sum_mix,))
    (
        block_out, tokens_grad, grad_first, grad_rate, grad_conv, grad_log, grad_bias,
        grad_outg, grad_second, grad_gate, grad_up, grad_down, grad_out,
    ) = early
    return (
        block_out, tokens_grad, grad_first, grad_mix, grad_rate, grad_conv, grad_log, grad_bias,
        grad_outg, grad_out, grad_second, grad_gate, grad_up, grad_down,
    )


def spread(
    tokens, seq_lengths, first_gain, mix_weight, rate_weight, conv_weight, decay_log, decay_bias,
    out_gain, out_weight, second_gain, gate_weight, up_weight, down_weight, cotangent,
):
    rows = tokens.shape[0]
    capacity = rows * lax.axis_size("tensor")
    here = lax.axis_index("tensor")
    gather = lambda v, axis=0: lax.all_gather(v, "tensor", axis=axis, tiled=True)
    scatter = lambda v, axis=0: lax.psum_scatter(
        v.astype(LOW), "tensor", scatter_dimension=axis, tiled=True
    )
    inputs = tokens.astype(F32)
    first_scale = norm_parts(inputs)
    token_rows = gather(tokens)
    gate_w, up_w, down_w = gather(gate_weight, 1), gather(up_weight, 1), gather(down_weight)
    segment, live_all = layout(seq_lengths[0], capacity)
    live = lax.dynamic_slice_in_dim(live_all, here * rows, rows, 0)
    marks, line = tables(segment)
    weights = mixer_weights(
        mix_weight, rate_weight, first_gain, decay_log, decay_bias, conv_weight, out_gain
    )
    heads = decay_log.shape[0]
    state = jnp.zeros((heads, DK, DV), F32)
    tail = jnp.zeros((PRIOR, heads * LANES), F32)
    mixed, kept, state, tail = mixer_fwd(
        jnp.ones((1, 1), F32), token_rows, token_rows, marks, line, weights, state, tail, (), 0
    )
    first_rows, kept = kept[0], kept[1:]
    residual = inputs + live * scatter(wide_dot(mixed, out_weight)).astype(F32)
    out_grad = cotangent.astype(F32)
    block_out, residual_grad, second_part, pieces = feed_forward(
        residual, live, second_gain, gate_w, up_w, down_w, out_grad
    )
    second_low, hidden, ffn_grad, gate_grad, up_grad = pieces
    attn_grad = gather((live * residual_grad).astype(LOW))
    grad_gate = scatter(cross(second_low, gate_grad), 1)
    grad_up = scatter(cross(second_low, up_grad), 1)
    grad_down = scatter(cross(hidden, ffn_grad))
    dmixed = back_dot(attn_grad, out_weight).astype(LOW)
    grad_out = cross(mixed, attn_grad).astype(LOW)
    part = mixer_bwd(dmixed, marks, line, conv_weight, out_gain[None], kept, 0, 1)
    dproj = part[0]
    dprep, dtaps, dgain = merge_back([part], heads)
    rates_grad, grad_log, grad_bias = rates_back(kept[1], decay_log, decay_bias, segment, dprep)
    rates_low = rates_grad.astype(LOW)
    grad_mix = cross(first_rows, dproj).astype(LOW)
    grad_rate = cross(first_rows, rates_low)
    first_sum = scatter(back_dot(dproj, mix_weight) + back_dot(rates_low, rate_weight))
    input_part, first_gain_part = norm_back(inputs, first_scale, first_gain, first_sum.astype(F32))
    tokens_grad = (residual_grad + input_part).astype(LOW)
    grad_rate, grad_conv, grad_log, grad_bias = lax.psum(
        (grad_rate, dtaps, grad_log, grad_bias), "dp"
    )
    grad_first, grad_outg, grad_second = lax.psum(
        (first_gain_part, dgain, second_part), ("dp", "tensor")
    )
    grad_mix, grad_out, grad_gate, grad_up, grad_down = (
        g.astype(F32) for g in lax.psum((grad_mix, grad_out, grad_gate, grad_up, grad_down), "dp")
    )
    return (
        block_out, tokens_grad, grad_first, grad_mix, grad_rate, grad_conv, grad_log, grad_bias,
        grad_outg, grad_out, grad_second, grad_gate, grad_up, grad_down,
    )


def solution(mesh):
    placed = (
        P(("dp", "tensor"), None),
        P("dp", None),
        P(),
        P(None, "tensor"),
        P(None, "tensor"),
        P(None, "tensor"),
        P("tensor"),
        P("tensor"),
        P(),
        P("tensor", None),
        P(),
        P(None, "tensor"),
        P(None, "tensor"),
        P("tensor", None),
        P(("dp", "tensor"), None),
    )
    outer = mesh.shape["dp"]
    two = mesh.shape["tensor"] == 2 and outer >= 4 and outer & (outer - 1) == 0
    return jax.shard_map(
        paired if two else spread,
        mesh=mesh,
        in_specs=placed,
        out_specs=(
            P(("dp", "tensor"), None),
            P(("dp", "tensor"), None),
            P(),
            P(None, "tensor"),
            P(None, "tensor"),
            P(None, "tensor"),
            P("tensor"),
            P("tensor"),
            P(),
            P("tensor", None),
            P(),
            P(None, "tensor"),
            P(None, "tensor"),
            P("tensor", None),
        ),
        check_vma=False,
    )
```

```python
from functools import partial

import jax
import jax.numpy as jnp
from jax import lax
from jax.experimental import pallas as pl
from jax.experimental.pallas import tpu as pltpu
from jax.sharding import PartitionSpec as P

DK = 128
DV = 256
CONV = 4
CHUNK = 128
LANES = 2 * DK + DV
WIDE = LANES + DV
BASE = 8
PRIOR = 16
F32 = jnp.float32
LOW = jnp.bfloat16


def dot(a, b):
    return lax.dot_general(a, b, (((1,), (0,)), ((), ())), preferred_element_type=F32)


def dot_rows(a, b):
    return lax.dot_general(a, b, (((1,), (1,)), ((), ())), preferred_element_type=F32)


def dot_cols(a, b):
    return lax.dot_general(a, b, (((0,), (0,)), ((), ())), preferred_element_type=F32)


def halves(a):
    high = a.astype(LOW)
    return high, (a - high.astype(F32)).astype(LOW)


def unit_lower_inverse(lows):
    size = lows[0].shape[0]
    row = lax.broadcasted_iota(jnp.int32, (size, size), 0)
    col = lax.broadcasted_iota(jnp.int32, (size, size), 1)
    eye = (row == col).astype(F32)
    near = (row // BASE) == (col // BASE)
    first = [jnp.where(near, -a, 0.0) for a in lows]
    powers = [p.astype(LOW) for p in first]
    inverse = [eye + p for p in first]
    span = 2
    while span < BASE:
        powers = [dot(p, p).astype(LOW) for p in powers]
        inverse = [t + dot(p, t.astype(LOW)) for p, t in zip(powers, inverse)]
        span *= 2
    span = BASE
    while span < size:
        band = ((row // (2 * span)) == (col // (2 * span))) & ((row // span) > (col // span))
        held = [t.astype(LOW) for t in inverse]
        moved = [dot(jnp.where(band, a, 0.0).astype(LOW), t).astype(LOW) for a, t in zip(lows, held)]
        inverse = [t - dot(h, m) for t, h, m in zip(inverse, held, moved)]
        span *= 2
    parts = [halves(t) for t in inverse]
    news = []
    for a, t, (t_high, t_low) in zip(lows, inverse, parts):
        a_high, a_low = halves(a)
        left = eye - t - (dot(a_high, t_high) + (dot(a_high, t_low) + dot(a_low, t_high)))
        news.append(t + dot(t_high, left.astype(LOW)))
    return news


def masks(marks, line):
    size = marks.shape[0]
    row = lax.broadcasted_iota(jnp.int32, (size, size), 0)
    col = lax.broadcasted_iota(jnp.int32, (size, size), 1)
    same = marks[:, 6:7] == line[0:1, :]
    return (row >= col) & same, (row > col) & same


def col_of(vals, kind, head, heads):
    at = kind * heads + head
    return vals[:, at : at + 1]


def rate_terms(logits, params, marks, heads):
    size = logits.shape[0]
    row = lax.broadcasted_iota(jnp.int32, (size, size), 0)
    col = lax.broadcasted_iota(jnp.int32, (size, size), 1)
    until = (row >= col).astype(LOW)
    shifted = logits + params[0:1, :]
    soft = jnp.maximum(shifted, 0.0) + jnp.log1p(jnp.exp(-jnp.abs(shifted)))
    decay = params[1:2, :] * soft
    high, rest = halves(decay)
    middle, small = halves(decay - high.astype(F32))
    grown = dot(until, high) + (dot(until, middle) + dot(until, small))
    start = jnp.exp(grown) * marks[:, 7:8]
    last = jnp.exp(grown[size - 1 : size, :] - grown) * marks[:, 8:9]
    lane = lax.broadcasted_iota(jnp.int32, logits.shape, 1)
    packed = pltpu.roll(logits, 4 * heads, 1)
    packed = jnp.where(lane < 4 * heads, pltpu.roll(last, 2 * heads, 1), packed)
    packed = jnp.where(lane < 3 * heads, pltpu.roll(start, heads, 1), packed)
    packed = jnp.where(lane < 2 * heads, grown, packed)
    packed = jnp.where(lane < heads, sigmoid(logits), packed)
    return packed, grown.T[heads : 2 * heads]


def sigmoid(x):
    return 1.0 / (1.0 + jnp.exp(-x))


def conv_sum(ext, cols, taps, at):
    size = cols.shape[0]
    total = ext[PRIOR : PRIOR + size, at : at + LANES] * taps[CONV - 1 : CONV, at : at + LANES]
    for back in range(1, CONV):
        moved = ext[PRIOR - back : PRIOR - back + size, at : at + LANES]
        tap = taps[CONV - 1 - back : CONV - back, at : at + LANES]
        total = total + (cols[:, back - 1 : back] * moved) * tap
    return total


def fwd_kernel(pick_ref, own_ref, got_ref, marks_ref, line_ref, mix_ref, rate_ref, first_ref, params_ref, taps_ref,
               gain_ref, state_in, tail_in, *refs):
    (mixed_ref, first_out, proj_ref, vals_ref, rows_ref, s_ref, t_ref, f_ref, o_ref,
     state, tail, ext) = refs[-12:]
    heads = state.shape[0]
    size = CHUNK

    @pl.when(pl.program_id(0) == 0)
    def _():
        state[...] = state_in[...]
        tail[...] = tail_in[...]

    hs = range(heads)
    marks = marks_ref[...]
    pick = pick_ref[0, 0]
    x = pick * own_ref[...].astype(F32) + (1.0 - pick) * got_ref[...].astype(F32)
    first = x * lax.rsqrt(jnp.mean(x * x, axis=1, keepdims=True) + 1e-05) * first_ref[...]
    first = first.astype(LOW)
    first_out[...] = first
    vals, grown = rate_terms(dot(first, rate_ref[...]), params_ref[...], marks, heads)
    vals_ref[...] = vals
    rows_ref[0:heads, :] = grown
    within, strict = masks(marks, line_ref[...])
    ext[0:PRIOR, :] = tail[...]
    for h in hs:
        at = h * LANES
        proj = dot(first, mix_ref[:, h * WIDE : (h + 1) * WIDE])
        proj_ref[:, h * WIDE : (h + 1) * WIDE] = proj
        ext[PRIOR : PRIOR + size, at : at + LANES] = proj[:, :LANES]
        tail[:, at : at + LANES] = proj[size - PRIOR :, :LANES]
    qs, ks, vs, betas, starts, lasts, fades = [], [], [], [], [], [], []
    for h in hs:
        summed = conv_sum(ext, marks, taps_ref, h * LANES)
        act = summed * sigmoid(summed)
        q = act[:, :DK]
        k = act[:, DK : 2 * DK]
        qs.append(q * (lax.rsqrt(jnp.sum(q * q, axis=1, keepdims=True) + 1e-06) * DK ** (-0.5)))
        ks.append(k * lax.rsqrt(jnp.sum(k * k, axis=1, keepdims=True) + 1e-06))
        vs.append(act[:, 2 * DK :])
        betas.append(col_of(vals, 0, h, heads))
        starts.append(col_of(vals, 2, h, heads))
        lasts.append(col_of(vals, 3, h, heads))
        spread = col_of(vals, 1, h, heads) - grown[h : h + 1, :]
        fades.append(jnp.exp(jnp.where(within, spread, -1e9)))
    stacks = [jnp.concatenate([q, k], axis=0).astype(LOW) for q, k in zip(qs, ks)]
    klows = [s[size:] for s in stacks]
    inner = [dot_rows(s, k) for s, k in zip(stacks, klows)]
    scores = [(i[:size] * m).astype(LOW) for i, m in zip(inner, fades)]
    lows = [jnp.where(strict, b * (i[size:] * m), 0.0) for b, i, m in zip(betas, inner, fades)]
    solve = [t.astype(LOW) for t in unit_lower_inverse(lows)]
    olds = [state[h] for h in hs]
    held = [s.astype(LOW) for s in olds]
    reads = [dot(q, s) for q, s in zip(stacks, held)]
    right = [(b * (v - e * r[size:])).astype(LOW) for b, v, e, r in zip(betas, vs, starts, reads)]
    fresh = [dot(t, x).astype(LOW) for t, x in zip(solve, right)]
    ends = [(l * k).astype(LOW) for l, k in zip(lasts, ks)]
    grows = [dot_cols(k, f) for k, f in zip(ends, fresh)]
    for h in hs:
        state[h] = starts[h][size - 1 : size, :] * olds[h] + grows[h]
    outs = [e * r[:size] + dot(p, f) for e, r, p, f in zip(starts, reads, scores, fresh)]
    gain = gain_ref[...]
    for h in hs:
        o = outs[h]
        gate = proj_ref[:, h * WIDE + LANES : (h + 1) * WIDE]
        scaled = o * lax.rsqrt(jnp.mean(o * o, axis=1, keepdims=True) + 1e-05) * gain
        mixed_ref[:, h * DV : (h + 1) * DV] = (scaled * (gate * sigmoid(gate))).astype(LOW)
        s_ref[0, h] = held[h]
        t_ref[0, h] = solve[h]
        f_ref[:, h * DV : (h + 1) * DV] = fresh[h]
        o_ref[:, h * DV : (h + 1) * DV] = o.astype(LOW)


def fold(x):
    return jnp.sum(x.reshape(x.shape[0] // 8, 8, x.shape[1]), axis=0)


def bwd_kernel(dmix_ref, prev_ref, proj_ref, marks_ref, line_ref, vals_ref, rows_ref, taps_ref, gain_ref,
               s_ref, t_ref, f_ref, o_ref,
               dproj_ref, dcols_ref, drows_ref, dtaps_ref, dgain_ref, dstate, ext, after,
               *, first, total_heads):
    heads = dstate.shape[0]
    size = CHUNK

    @pl.when(pl.program_id(0) == 0)
    def _():
        dstate[...] = jnp.zeros_like(dstate)
        after[...] = jnp.zeros_like(after)
        dtaps_ref[...] = jnp.zeros_like(dtaps_ref)
        dgain_ref[...] = jnp.zeros_like(dgain_ref)

    marks = marks_ref[...]
    vals = vals_ref[...]
    rows = rows_ref[...]
    within, strict = masks(marks, line_ref[...])
    gain = gain_ref[...]
    for h in range(heads):
        at = h * LANES
        ext[0:PRIOR, at : at + LANES] = prev_ref[:, h * WIDE : h * WIDE + LANES].astype(F32)
        ext[PRIOR : PRIOR + size, at : at + LANES] = proj_ref[:, h * WIDE : h * WIDE + LANES].astype(F32)
    hs = range(heads)
    summed = [conv_sum(ext, marks, taps_ref, h * LANES) for h in hs]
    sig = [sigmoid(s) for s in summed]
    act = [s * g for s, g in zip(summed, sig)]
    slope = [g * (1.0 + s * (1.0 - g)) for s, g in zip(summed, sig)]
    rq = [lax.rsqrt(jnp.sum(a[:, :DK] * a[:, :DK], axis=1, keepdims=True) + 1e-06) for a in act]
    rk = [lax.rsqrt(jnp.sum(a[:, DK : 2 * DK] * a[:, DK : 2 * DK], axis=1, keepdims=True) + 1e-06) for a in act]
    qn = [a[:, :DK] * r for a, r in zip(act, rq)]
    ks = [a[:, DK : 2 * DK] * r for a, r in zip(act, rk)]
    vs = [a[:, 2 * DK :] for a in act]
    betas = [col_of(vals, 0, first + h, total_heads) for h in hs]
    starts = [col_of(vals, 2, first + h, total_heads) for h in hs]
    lasts = [col_of(vals, 3, first + h, total_heads) for h in hs]
    fades = [
        jnp.exp(jnp.where(within, col_of(vals, 1, first + h, total_heads) - rows[first + h : first + h + 1, :], -1e9)) for h in hs
    ]
    stacks = [jnp.concatenate([q * DK ** (-0.5), k], axis=0).astype(LOW) for q, k in zip(qn, ks)]
    qlows = [s[:size] for s in stacks]
    klows = [s[size:] for s in stacks]
    inner = [dot_rows(s, k) for s, k in zip(stacks, klows)]
    scores = [i[:size] * m for i, m in zip(inner, fades)]
    pairs = [jnp.where(strict, i[size:] * m, 0.0) for i, m in zip(inner, fades)]
    held = [s_ref[0, h] for h in hs]
    reads = [dot(q, s) for q, s in zip(stacks, held)]
    douts = []
    for h in hs:
        o = o_ref[:, h * DV : (h + 1) * DV].astype(F32)
        gate = proj_ref[:, h * WIDE + LANES : (h + 1) * WIDE].astype(F32)
        dmix = dmix_ref[:, h * DV : (h + 1) * DV].astype(F32)
        r = lax.rsqrt(jnp.mean(o * o, axis=1, keepdims=True) + 1e-05)
        g = sigmoid(gate)
        on = o * r
        u = dmix * (gate * g)
        dgain_ref[...] += fold(u * on)
        dgate = (dmix * on * gain) * (g * (1.0 + gate * (1.0 - g)))
        dproj_ref[:, h * WIDE + LANES : (h + 1) * WIDE] = dgate.astype(LOW)
        w = u * gain
        douts.append(r * (w - on * jnp.mean(w * on, axis=1, keepdims=True)))
    dlows = [d.astype(LOW) for d in douts]
    dnexts = [dstate[h] for h in hs]
    dheld = [d.astype(LOW) for d in dnexts]
    ends = [(l * k).astype(LOW) for l, k in zip(lasts, ks)]
    solve = [t_ref[0, h] for h in hs]
    fresh = [f_ref[:, h * DV : (h + 1) * DV] for h in hs]
    dfresh = [dot_cols(p.astype(LOW), d) + dot(k, s) for p, d, k, s in zip(scores, dlows, ends, dheld)]
    dright = [dot_cols(t, d.astype(LOW)) for t, d in zip(solve, dfresh)]
    outer = [
        dot_rows(jnp.concatenate([d, x.astype(LOW)], axis=0), f)
        for d, x, f in zip(dlows, dright, fresh)
    ]
    scaled = [b * x for b, x in zip(betas, dright)]
    dreads = [
        jnp.concatenate([e * d, -e * x], axis=0).astype(LOW) for e, d, x in zip(starts, douts, scaled)
    ]
    for h in hs:
        dstate[h] = starts[h][size - 1 : size, :] * dnexts[h] + dot_cols(stacks[h], dreads[h])
    dqk = [dot_rows(d, s) for d, s in zip(dreads, held)]
    dend = [dot_rows(f, s) for f, s in zip(fresh, dheld)]
    last_row = lax.broadcasted_iota(jnp.int32, (size, 1), 0) == size - 1
    dscore = [o[:size] * m for o, m in zip(outer, fades)]
    dpair = [-o[size:] for o in outer]
    dinner = [jnp.where(strict, b * d * m, 0.0) for b, d, m in zip(betas, dpair, fades)]
    dq_in = [dot(d.astype(LOW), k) for d, k in zip(dscore, klows)]
    dk_in = [
        dot_cols(d.astype(LOW), q) + dot((i + i.T).astype(LOW), k)
        for d, q, i, k in zip(dscore, qlows, dinner, klows)
    ]
    for h in hs:
        e, b, dr, y, z = starts[h], betas[h], dright[h], reads[h][:size], reads[h][size:]
        weights = scores[h] * outer[h][:size] + b * pairs[h] * dpair[h]
        dbeta = jnp.sum(dr * (vs[h] - e * z), axis=1, keepdims=True) + jnp.sum(
            dpair[h] * pairs[h], axis=1, keepdims=True
        )
        dstart = jnp.sum(douts[h] * y - scaled[h] * z, axis=1, keepdims=True)
        through = jnp.sum(dnexts[h] * held[h].astype(F32))
        dstart = dstart + jnp.where(last_row, through, 0.0)
        dlast = jnp.sum(ks[h] * dend[h], axis=1, keepdims=True)
        at = h
        dcols_ref[:, at : at + 1] = dbeta
        dcols_ref[:, heads + at : heads + at + 1] = jnp.sum(weights, axis=1, keepdims=True)
        dcols_ref[:, 2 * heads + at : 2 * heads + at + 1] = dstart
        dcols_ref[:, 3 * heads + at : 3 * heads + at + 1] = dlast
        drows_ref[h : h + 1, :] = jnp.sum(weights, axis=0, keepdims=True)
    for h in hs:
        dq = dqk[h][:size] + dq_in[h]
        dk = dqk[h][size:] + dk_in[h] + lasts[h] * dend[h]
        dv = scaled[h]
        dq = (rq[h] * DK ** (-0.5)) * (dq - qn[h] * jnp.sum(dq * qn[h], axis=1, keepdims=True))
        dk = rk[h] * (dk - ks[h] * jnp.sum(dk * ks[h], axis=1, keepdims=True))
        at = h * LANES
        dsum = jnp.concatenate([dq, dk, dv], axis=1) * slope[h]
        after[0:size, at : at + LANES] = dsum
        here = slice(at, at + LANES)
        dproj = dsum * taps_ref[CONV - 1 : CONV, here]
        dtaps_ref[CONV - 1, :, here] += fold(dsum * ext[PRIOR : PRIOR + size, here])
        for back in range(1, CONV):
            moved = ext[PRIOR - back : PRIOR - back + size, here]
            dtaps_ref[CONV - 1 - back, :, here] += fold((marks[:, back - 1 : back] * moved) * dsum)
            later = after[back : back + size, here]
            dproj = dproj + (marks[:, 2 + back : 3 + back] * later) * taps_ref[CONV - 1 - back : CONV - back, here]
        dproj_ref[:, h * WIDE : h * WIDE + LANES] = dproj.astype(LOW)
        after[size : size + 8, here] = dsum[0:8]


PARAMS = pltpu.CompilerParams(
    dimension_semantics=("arbitrary",), vmem_limit_bytes=56 * 1024 * 1024
)


def fixed(shape):
    return pl.BlockSpec(shape, lambda i: (0,) * len(shape), pipeline_mode=pl.Buffered(1))


def cost(total, heads):
    return pl.CostEstimate(
        flops=10_000_000 * total * heads, bytes_accessed=total * heads * 8192, transcendentals=0
    )


def mixer_fwd(pick, x, got, marks, line, weights, state, tail, kept, at):
    mix_w, rate_w, first_gain, params, taps, gain = weights
    total, width = line.shape[1], x.shape[1]
    heads = mix_w.shape[1] // WIDE
    chunks = total // CHUNK
    rows_at = lambda i: (at + i, 0)
    blocks_at = lambda i: (at + i, 0, 0, 0)
    whole = [
        (pl.BlockSpec((CHUNK, width), rows_at), (total, width), LOW),
        (pl.BlockSpec((CHUNK, heads * WIDE), rows_at), (total, heads * WIDE), F32),
        (pl.BlockSpec((CHUNK, 128), rows_at), (total, 128), F32),
        (pl.BlockSpec((8, CHUNK), lambda i: (0, at + i)), (8, total), F32),
        (pl.BlockSpec((1, heads, DK, DV), blocks_at), (chunks, heads, DK, DV), LOW),
        (pl.BlockSpec((1, heads, CHUNK, CHUNK), blocks_at), (chunks, heads, CHUNK, CHUNK), LOW),
        (pl.BlockSpec((CHUNK, heads * DV), rows_at), (total, heads * DV), LOW),
        (pl.BlockSpec((CHUNK, heads * DV), rows_at), (total, heads * DV), LOW),
    ]
    in_specs = [
        pl.BlockSpec(memory_space=pltpu.SMEM),
        pl.BlockSpec((CHUNK, width), lambda i: (i, 0)),
        pl.BlockSpec((CHUNK, width), lambda i: (i, 0)),
        pl.BlockSpec((CHUNK, marks.shape[1]), rows_at),
        pl.BlockSpec((8, CHUNK), lambda i: (0, at + i)),
        fixed(mix_w.shape),
        fixed(rate_w.shape),
        fixed(first_gain.shape),
        fixed(params.shape),
        fixed(taps.shape),
        fixed(gain.shape),
        fixed((heads, DK, DV)),
        fixed((PRIOR, heads * LANES)),
    ]
    out = pl.pallas_call(
        fwd_kernel,
        grid=(x.shape[0] // CHUNK,),
        in_specs=in_specs + [pl.BlockSpec(memory_space=pl.ANY)] * len(kept),
        out_specs=[pl.BlockSpec((CHUNK, heads * DV), lambda i: (i, 0))]
        + [w[0] for w in whole]
        + [
            pl.BlockSpec((heads, DK, DV), lambda i: (0, 0, 0)),
            pl.BlockSpec((PRIOR, heads * LANES), lambda i: (0, 0)),
        ],
        out_shape=[jax.ShapeDtypeStruct((x.shape[0], heads * DV), LOW)]
        + [jax.ShapeDtypeStruct(w[1], w[2]) for w in whole]
        + [
            jax.ShapeDtypeStruct((heads, DK, DV), F32),
            jax.ShapeDtypeStruct((PRIOR, heads * LANES), F32),
        ],
        scratch_shapes=[pltpu.VMEM((CHUNK + PRIOR, heads * LANES), F32)],
        input_output_aliases={len(in_specs) + n: 1 + n for n in range(len(kept))},
        compiler_params=PARAMS,
        cost_estimate=cost(x.shape[0], heads),
        name="mixer_forward",
    )(pick, x, got, marks, line, mix_w, rate_w, first_gain, params, taps, gain, state, tail, *kept)
    return out[0], out[1:9], out[9], out[10]


def mixer_bwd(dmixed, marks, line, taps, gain, kept, group, groups):
    proj, vals, rows, states, solves, fresh, outs = kept
    total = proj.shape[0]
    whole = proj.shape[1] // WIDE
    heads = whole // groups
    chunks = total // CHUNK
    per = CHUNK // PRIOR
    at = lambda i: chunks - 1 - i
    return pl.pallas_call(
        partial(bwd_kernel, first=group * heads, total_heads=whole),
        grid=(chunks,),
        in_specs=[
            pl.BlockSpec((CHUNK, heads * DV), lambda i: (at(i), group)),
            pl.BlockSpec((PRIOR, heads * WIDE), lambda i: (jnp.maximum(at(i) * per - 1, 0), group)),
            pl.BlockSpec((CHUNK, heads * WIDE), lambda i: (at(i), group)),
            pl.BlockSpec((CHUNK, marks.shape[1]), lambda i: (at(i), 0)),
            pl.BlockSpec((8, CHUNK), lambda i: (0, at(i))),
            pl.BlockSpec((CHUNK, 128), lambda i: (at(i), 0)),
            pl.BlockSpec((rows.shape[0], CHUNK), lambda i: (0, at(i))),
            pl.BlockSpec((CONV, heads * LANES), lambda i: (0, group)),
            pl.BlockSpec((1, DV), lambda i: (0, 0)),
            pl.BlockSpec((1, heads, DK, DV), lambda i: (at(i), group, 0, 0)),
            pl.BlockSpec((1, heads, CHUNK, CHUNK), lambda i: (at(i), group, 0, 0)),
            pl.BlockSpec((CHUNK, heads * DV), lambda i: (at(i), group)),
            pl.BlockSpec((CHUNK, heads * DV), lambda i: (at(i), group)),
        ],
        out_specs=[
            pl.BlockSpec((CHUNK, heads * WIDE), lambda i: (at(i), 0)),
            pl.BlockSpec((CHUNK, 4 * heads), lambda i: (at(i), 0)),
            pl.BlockSpec((8, CHUNK), lambda i: (0, at(i))),
            pl.BlockSpec((CONV, 8, heads * LANES), lambda i: (0, 0, 0)),
            pl.BlockSpec((8, DV), lambda i: (0, 0)),
        ],
        out_shape=[
            jax.ShapeDtypeStruct((total, heads * WIDE), LOW),
            jax.ShapeDtypeStruct((total, 4 * heads), F32),
            jax.ShapeDtypeStruct((8, total), F32),
            jax.ShapeDtypeStruct((CONV, 8, heads * LANES), F32),
            jax.ShapeDtypeStruct((8, DV), F32),
        ],
        scratch_shapes=[
            pltpu.VMEM((heads, DK, DV), F32),
            pltpu.VMEM((CHUNK + PRIOR, heads * LANES), F32),
            pltpu.VMEM((CHUNK + 8, heads * LANES), F32),
        ],
        compiler_params=PARAMS,
        cost_estimate=cost(total, heads),
        name="mixer_backward",
    )(dmixed, proj, proj, marks, line, vals, rows, taps, gain, states, solves, fresh, outs)


def merge_back(parts, heads):
    each = heads // len(parts)
    cut = [[p[1][:, k * each : (k + 1) * each] for p in parts] for k in range(4)]
    dbeta, dgrown, dstart, dlast = [jnp.concatenate(c, axis=1) for c in cut]
    dgrown = dgrown - jnp.concatenate([p[2][:each] for p in parts], axis=0).T
    dtaps = jnp.concatenate([jnp.sum(p[3], axis=1) for p in parts], axis=1)
    dgain = sum(jnp.sum(p[4], axis=0) for p in parts)
    return (dbeta, dgrown, dstart, dlast), dtaps, dgain


def prep(rates, decay_log, decay_bias, segment):
    total = rates.shape[0]
    heads = decay_log.shape[0]
    chunks = total // CHUNK
    pieces = rates.reshape(total, heads, 2)
    beta = jax.nn.sigmoid(pieces[..., 0])
    decay = -jnp.exp(decay_log) * jax.nn.softplus(pieces[..., 1] + decay_bias)
    order = jnp.arange(CHUNK)
    until = (order[:, None] >= order[None, :]).astype(F32)
    grown = jnp.einsum(
        "ij,njh->nih", until, decay.reshape(chunks, CHUNK, heads), precision=lax.Precision.HIGHEST
    )
    seg = segment.reshape(chunks, CHUNK)
    before = jnp.concatenate([jnp.full((1,), -1, jnp.int32), seg[:-1, -1]])
    carried = (seg == before[:, None])[:, :, None]
    start = jnp.where(carried, jnp.exp(grown), 0.0)
    ending = (seg == seg[:, -1:])[:, :, None]
    last = jnp.where(ending, jnp.exp(jnp.where(ending, grown[:, -1:] - grown, 0.0)), 0.0)
    return (
        beta,
        grown.reshape(total, heads),
        start.reshape(total, heads),
        last.reshape(total, heads),
    )


def tables(segment):
    total = segment.shape[0]
    seg = segment.reshape(-1, CHUNK)
    before = jnp.concatenate([jnp.full((1,), -1, jnp.int32), seg[:-1, -1]])
    marks = []
    for back in range(1, CONV):
        prior = jnp.pad(segment, (back, 0), constant_values=-1)[:total]
        marks.append(prior == segment)
    for back in range(1, CONV):
        later = jnp.pad(segment, (0, back), constant_values=-1)[back:]
        marks.append(later == segment)
    marks.append(segment)
    marks.append((seg == before[:, None]).reshape(total))
    marks.append((seg == seg[:, -1:]).reshape(total))
    marks += [jnp.zeros((total,), F32)] * 7
    marks = jnp.stack([m.astype(F32) for m in marks], axis=1)
    return marks, jnp.broadcast_to(segment.astype(F32)[None], (8, total))


def mixer_weights(mix_w, rate_w, first_gain, decay_log, decay_bias, taps, gain):
    heads = decay_log.shape[0]
    paired_w = rate_w.reshape(-1, heads, 2)
    filled = jnp.concatenate([paired_w[..., 0], paired_w[..., 1]], axis=1)
    filled = jnp.pad(filled, ((0, 0), (0, 128 - 2 * heads)))
    params = jnp.zeros((8, 128), F32)
    params = params.at[0, heads : 2 * heads].set(decay_bias)
    params = params.at[1, heads : 2 * heads].set(-jnp.exp(decay_log))
    return mix_w, filled, first_gain[None], params, taps, gain[None]


def rates_back(vals, decay_log, decay_bias, segment, grads):
    heads = decay_log.shape[0]
    logits = vals[:, 4 * heads : 6 * heads].reshape(-1, 2, heads).transpose(0, 2, 1)
    rates = logits.reshape(-1, 2 * heads)
    back = jax.vjp(lambda r, l, b: prep(r, l, b, segment), rates, decay_log, decay_bias)[1]
    return back(grads)


def cross(left, right):
    return lax.dot_general(
        left, right, (((0,), (0,)), ((), ())), preferred_element_type=F32
    )


def wide_dot(left, right):
    return jnp.dot(left, right, preferred_element_type=F32)


def back_dot(grad, weight):
    return lax.dot_general(
        grad, weight, (((1,), (1,)), ((), ())), preferred_element_type=F32
    )


def norm_parts(value):
    return lax.rsqrt(jnp.mean(value * value, axis=-1, keepdims=True) + 1e-05)


def norm_back(value, scale, gain, grad):
    u = gain * grad
    part = scale * u - value * (scale * scale * scale) * jnp.mean(u * value, axis=-1, keepdims=True)
    return part, jnp.sum(grad * value * scale, axis=0)


def layout(lengths, capacity):
    bounds = jnp.cumsum(lengths)
    position = jnp.arange(capacity, dtype=jnp.int32)
    segment = jnp.sum((position[:, None] >= bounds[None, :]).astype(jnp.int32), axis=1)
    live = (position < bounds[-1]).astype(F32)[:, None]
    return segment, live


class Pair:
    def __init__(self, groups):
        self.here = lax.axis_index("tensor")
        self.core = lax.axis_index("dp") % 2
        self.side = (lax.axis_index("dp") // 2) % 2
        self.cores = [(i, i ^ 1) for i in range(groups)]
        self.sides = [(i, i ^ 2) for i in range(groups)]
        self.groups = groups

    def across(self, value):
        return lax.ppermute(value, "tensor", [(0, 1), (1, 0)])

    def beside(self, value):
        return lax.ppermute(value, "dp", self.cores)

    def along(self, value):
        return lax.ppermute(value, "dp", self.sides)

    def part(self, value, which):
        size = value.shape[0] // 2
        return lax.dynamic_slice_in_dim(value, which * size, size, 0)

    def join(self, mine, other, which):
        low = jnp.where(which == 0, mine, other)
        return jnp.concatenate([low, jnp.where(which == 0, other, mine)], axis=0)

    def halve(self, value):
        mine = self.part(value, self.core).astype(F32)
        got = self.beside(self.part(value, 1 - self.core)).astype(F32)
        return (mine + got).astype(LOW)

    def quarter(self, half):
        mine = self.part(half, self.side).astype(F32)
        got = self.along(self.part(half, 1 - self.side)).astype(F32)
        return (mine + got).astype(LOW)

    def sum(self, values, turn, alike=2):
        orders = []
        for c in range(alike):
            order = list(range(c, self.groups, alike))
            order = order[turn:] + order[:turn]
            orders.append(order)
        return lax.psum(values, "dp", axis_index_groups=orders)

    def halves(self, values):
        return [self.join(v, self.along(v), self.side) for v in values]

    def everywhere(self, value):
        step = 1
        while step < self.groups:
            value = value + lax.ppermute(value, "dp", [(i, i ^ step) for i in range(self.groups)])
            step *= 2
        return value

    def whole(self, values):
        return [self.join(v, self.beside(v), self.core).astype(F32) for v in values]


def feed_forward(residual, live, second_gain, gate_w, up_w, down_w, out_grad):
    scale = norm_parts(residual)
    second_low = (residual * scale * second_gain).astype(LOW)
    gate = wide_dot(second_low, gate_w)
    up = wide_dot(second_low, up_w)
    sigma = jax.nn.sigmoid(gate)
    gated = gate * sigma
    hidden = (gated * up).astype(LOW)
    block_out = (residual + live * wide_dot(hidden, down_w)).astype(LOW)
    ffn_grad = (live * out_grad).astype(LOW)
    hidden_grad = back_dot(ffn_grad, down_w)
    gate_grad = (hidden_grad * up * (sigma * (1.0 + gate * (1.0 - sigma)))).astype(LOW)
    up_grad = (hidden_grad * gated).astype(LOW)
    second_sum = back_dot(gate_grad, gate_w) + back_dot(up_grad, up_w)
    part, gain_part = norm_back(residual, scale, second_gain, second_sum)
    residual_grad = out_grad + part
    pieces = (second_low, hidden, ffn_grad, gate_grad, up_grad)
    return block_out, residual_grad, gain_part, pieces


def tied(*values):
    return lax.optimization_barrier(values)


def paired(
    tokens, seq_lengths, first_gain, mix_weight, rate_weight, conv_weight, decay_log, decay_bias,
    out_gain, out_weight, second_gain, gate_weight, up_weight, down_weight, cotangent,
):
    rows = tokens.shape[0]
    capacity = rows * 2
    move = Pair(lax.axis_size("dp"))
    here = move.here
    heads = decay_log.shape[0]
    cuts = 3 if rows % (3 * CHUNK) == 0 else 1
    piece = rows // cuts
    own = [tokens[j * piece : (j + 1) * piece] for j in range(cuts)]
    got = [move.across(own[0])]
    for j in range(1, cuts):
        got[-1], own[j] = tied(got[-1], own[j])
        got.append(move.across(own[j]))
    gate_src, up_src, down_src, last_got = tied(gate_weight, up_weight, down_weight, got[-1])
    got[-1] = last_got
    fetched = [
        move.across(move.part(move.part(w, move.core), move.side))
        for w in (gate_src, up_src, down_src)
    ]
    segment, live_all = layout(seq_lengths[0], capacity)
    live = lax.dynamic_slice_in_dim(live_all, here * rows, rows, 0)
    marks, line = tables(segment)
    weights = mixer_weights(
        mix_weight, rate_weight, first_gain, decay_log, decay_bias, conv_weight, out_gain
    )
    state = jnp.zeros((heads, DK, DV), F32)
    tail = jnp.zeros((PRIOR, heads * LANES), F32)
    first_half = (here == 0).astype(F32).reshape(1, 1)
    per = piece // CHUNK
    mixed, kept, attn_own, attn_got = [], (), [], []
    for p in range(2 * cuts):
        pick = first_half if p < cuts else 1.0 - first_half
        now, kept, state, tail = mixer_fwd(pick, own[p % cuts], got[p % cuts], marks, line, weights, state, tail, kept, p * per)
        mixed.append(now)
        if p == cuts:
            fetched, state = tied(fetched, state)
            fetched = [move.join(f, move.along(f), move.side) for f in fetched]
        if p > cuts:
            now, attn_got[-1] = tied(now, attn_got[-1])
            mixed[-1] = now
        if p >= cuts:
            low, high = wide_dot(mixed[p - cuts], out_weight), wide_dot(now, out_weight)
            attn_own.append(jnp.where(here == 0, low, high))
            attn_got.append(move.across(jnp.where(here == 0, high, low).astype(LOW)))
    fetched, mixed[-1] = tied(fetched, mixed[-1])
    others = [move.join(f, move.beside(f), move.core) for f in fetched]
    gate_w = jnp.concatenate([gate_weight, others[0]], axis=1)
    up_w = jnp.concatenate([up_weight, others[1]], axis=1)
    down_w = jnp.concatenate([down_weight, others[2]], axis=0)
    attn_got, gate_w, up_w, down_w = tied(attn_got, gate_w, up_w, down_w)
    attn = jnp.concatenate([a + g.astype(F32) for a, g in zip(attn_own, attn_got)], axis=0)
    first_rows, kept = kept[0], kept[1:]
    inputs = tokens.astype(F32)
    residual = inputs + live * attn

    width = gate_weight.shape[1]
    out_grad = cotangent.astype(F32)
    scale = norm_parts(residual)
    second_low = (residual * scale * second_gain).astype(LOW)
    gate = wide_dot(second_low, gate_w)
    up = wide_dot(second_low, up_w)
    sigma = jax.nn.sigmoid(gate)
    gated = gate * sigma
    hidden = (gated * up).astype(LOW)
    ffn_grad = (live * out_grad).astype(LOW)
    hidden_grad = back_dot(ffn_grad, down_w)
    gate_grad = (hidden_grad * up * (sigma * (1.0 + gate * (1.0 - sigma)))).astype(LOW)
    up_grad = (hidden_grad * gated).astype(LOW)
    grad_down = cross(hidden, ffn_grad).astype(LOW)
    down_halves = [move.halve(grad_down[:width]), move.halve(grad_down[width:])]
    gate_half = move.halve(cross(second_low, gate_grad).astype(LOW))
    up_half = move.halve(cross(second_low, up_grad).astype(LOW))
    gate_in, up_in, down_halves, gate_half, up_half = tied(
        gate_grad, up_grad, down_halves, gate_half, up_half
    )
    down_mine, down_sent = [move.quarter(d) for d in down_halves]
    gate_half, up_half = move.quarter(gate_half), move.quarter(up_half)
    down_sent = move.across(down_sent)
    gate_sent = move.across(gate_half[:, width:])
    up_sent = move.across(up_half[:, width:])
    second_sum = back_dot(gate_in, gate_w) + back_dot(up_in, up_w)
    part, second_part = norm_back(residual, scale, second_gain, second_sum)
    residual_grad = out_grad + part
    attn_low = (live * residual_grad).astype(LOW)
    attn_sent = move.across(attn_low)
    attn_low, hidden_in = tied(attn_low, hidden)
    block_out = (residual + live * wide_dot(hidden_in, down_w)).astype(LOW)
    mixed = jnp.concatenate(mixed, axis=0)
    gate_sum = gate_half[:, :width] + gate_sent
    up_sum = up_half[:, :width] + up_sent
    down_sum = down_mine + down_sent
    attn_sent, block_out, mixed = tied(attn_sent, block_out, mixed)
    attn_grad = move.join(attn_low, attn_sent, here)
    dmixed = back_dot(attn_grad, out_weight).astype(LOW)
    grad_out = move.quarter(move.halve(cross(mixed, attn_grad).astype(LOW)))

    dmixed, sums_ffn_in = tied(dmixed, (gate_sum, up_sum, down_sum, grad_out))
    sums_ffn = move.sum(sums_ffn_in, 0, 4)
    back = mixer_bwd(dmixed, marks, line, conv_weight, out_gain[None], kept, 0, 1)
    back, sums_ffn = tied(back, sums_ffn)
    dproj = back[0]
    dprep, dtaps, dgain = merge_back([back], heads)
    rates_grad, grad_log, grad_bias = rates_back(
        kept[1], decay_log, decay_bias, segment, dprep
    )
    rates_low = rates_grad.astype(LOW)

    def first_part(dproj, which):
        return back_dot(move.part(rates_low, which), rate_weight) + back_dot(
            move.part(dproj, which), mix_weight
        )

    theirs = first_part(dproj, 1 - here)
    theirs_low = theirs.astype(LOW)
    dproj, theirs_low = tied(dproj, theirs_low)
    sent = move.across(theirs_low)
    half = move.halve(cross(first_rows, dproj).astype(LOW))
    dproj, half = tied(dproj, half)
    (sum_mix,) = move.sum((half,), 1)
    sums_ffn = move.halves(sums_ffn)
    mine = first_part(dproj, here)
    grad_rate = cross(rates_low, first_rows)
    token_own = inputs
    token_other = jnp.concatenate(got, axis=0).astype(F32)
    first_scale = norm_parts(token_own)
    first_part_gain = jnp.sum(mine * token_own * first_scale, axis=0) + jnp.sum(
        theirs * token_other * norm_parts(token_other), axis=0
    )
    model = first_gain.shape[0]
    thin = jnp.concatenate([dgain, grad_log, grad_bias])
    thin = jnp.pad(thin, (0, model - thin.shape[0]))
    small = jnp.concatenate(
        [first_part_gain[None], second_part[None], thin[None], grad_rate, dtaps.reshape(-1, model)]
    )
    small = move.everywhere(small)
    gains = small[:3] + move.across(small[:3])
    grad_first, grad_second, grad_outg = gains[0], gains[1], gains[2, :DV]
    grad_log = small[2, DV : DV + heads]
    grad_bias = small[2, DV + heads : DV + 2 * heads]
    grad_rate = small[3 : 3 + 2 * heads].T
    grad_conv = small[3 + 2 * heads :].reshape(dtaps.shape)

    grad_gate, grad_up, grad_down, grad_out = move.whole(sums_ffn)
    sent, grad_gate, grad_up, grad_down, grad_out = tied(
        sent, grad_gate, grad_up, grad_down, grad_out
    )
    input_part, _ = norm_back(inputs, first_scale, first_gain, mine + sent.astype(F32))
    tokens_grad = (residual_grad + input_part).astype(LOW)
    early = (
        block_out, tokens_grad, grad_first, grad_rate, grad_conv, grad_log, grad_bias,
        grad_outg, grad_second, grad_gate, grad_up, grad_down, grad_out,
    )
    early, sum_mix = tied(early, sum_mix)
    (grad_mix,) = move.whole((sum_mix,))
    (
        block_out, tokens_grad, grad_first, grad_rate, grad_conv, grad_log, grad_bias,
        grad_outg, grad_second, grad_gate, grad_up, grad_down, grad_out,
    ) = early
    return (
        block_out, tokens_grad, grad_first, grad_mix, grad_rate, grad_conv, grad_log, grad_bias,
        grad_outg, grad_out, grad_second, grad_gate, grad_up, grad_down,
    )


def spread(
    tokens, seq_lengths, first_gain, mix_weight, rate_weight, conv_weight, decay_log, decay_bias,
    out_gain, out_weight, second_gain, gate_weight, up_weight, down_weight, cotangent,
):
    rows = tokens.shape[0]
    capacity = rows * lax.axis_size("tensor")
    here = lax.axis_index("tensor")
    gather = lambda v, axis=0: lax.all_gather(v, "tensor", axis=axis, tiled=True)
    scatter = lambda v, axis=0: lax.psum_scatter(
        v.astype(LOW), "tensor", scatter_dimension=axis, tiled=True
    )
    inputs = tokens.astype(F32)
    first_scale = norm_parts(inputs)
    token_rows = gather(tokens)
    gate_w, up_w, down_w = gather(gate_weight, 1), gather(up_weight, 1), gather(down_weight)
    segment, live_all = layout(seq_lengths[0], capacity)
    live = lax.dynamic_slice_in_dim(live_all, here * rows, rows, 0)
    marks, line = tables(segment)
    weights = mixer_weights(
        mix_weight, rate_weight, first_gain, decay_log, decay_bias, conv_weight, out_gain
    )
    heads = decay_log.shape[0]
    state = jnp.zeros((heads, DK, DV), F32)
    tail = jnp.zeros((PRIOR, heads * LANES), F32)
    mixed, kept, state, tail = mixer_fwd(
        jnp.ones((1, 1), F32), token_rows, token_rows, marks, line, weights, state, tail, (), 0
    )
    first_rows, kept = kept[0], kept[1:]
    residual = inputs + live * scatter(wide_dot(mixed, out_weight)).astype(F32)
    out_grad = cotangent.astype(F32)
    block_out, residual_grad, second_part, pieces = feed_forward(
        residual, live, second_gain, gate_w, up_w, down_w, out_grad
    )
    second_low, hidden, ffn_grad, gate_grad, up_grad = pieces
    attn_grad = gather((live * residual_grad).astype(LOW))
    grad_gate = scatter(cross(second_low, gate_grad), 1)
    grad_up = scatter(cross(second_low, up_grad), 1)
    grad_down = scatter(cross(hidden, ffn_grad))
    dmixed = back_dot(attn_grad, out_weight).astype(LOW)
    grad_out = cross(mixed, attn_grad).astype(LOW)
    part = mixer_bwd(dmixed, marks, line, conv_weight, out_gain[None], kept, 0, 1)
    dproj = part[0]
    dprep, dtaps, dgain = merge_back([part], heads)
    rates_grad, grad_log, grad_bias = rates_back(kept[1], decay_log, decay_bias, segment, dprep)
    rates_low = rates_grad.astype(LOW)
    grad_mix = cross(first_rows, dproj).astype(LOW)
    grad_rate = cross(first_rows, rates_low)
    first_sum = scatter(back_dot(dproj, mix_weight) + back_dot(rates_low, rate_weight))
    input_part, first_gain_part = norm_back(inputs, first_scale, first_gain, first_sum.astype(F32))
    tokens_grad = (residual_grad + input_part).astype(LOW)
    grad_rate, grad_conv, grad_log, grad_bias = lax.psum(
        (grad_rate, dtaps, grad_log, grad_bias), "dp"
    )
    grad_first, grad_outg, grad_second = lax.psum(
        (first_gain_part, dgain, second_part), ("dp", "tensor")
    )
    grad_mix, grad_out, grad_gate, grad_up, grad_down = (
        g.astype(F32) for g in lax.psum((grad_mix, grad_out, grad_gate, grad_up, grad_down), "dp")
    )
    return (
        block_out, tokens_grad, grad_first, grad_mix, grad_rate, grad_conv, grad_log, grad_bias,
        grad_outg, grad_out, grad_second, grad_gate, grad_up, grad_down,
    )


def solution(mesh):
    placed = (
        P(("dp", "tensor"), None),
        P("dp", None),
        P(),
        P(None, "tensor"),
        P(None, "tensor"),
        P(None, "tensor"),
        P("tensor"),
        P("tensor"),
        P(),
        P("tensor", None),
        P(),
        P(None, "tensor"),
        P(None, "tensor"),
        P("tensor", None),
        P(("dp", "tensor"), None),
    )
    outer = mesh.shape["dp"]
    two = mesh.shape["tensor"] == 2 and outer >= 4 and outer & (outer - 1) == 0
    return jax.shard_map(
        paired if two else spread,
        mesh=mesh,
        in_specs=placed,
        out_specs=(
            P(("dp", "tensor"), None),
            P(("dp", "tensor"), None),
            P(),
            P(None, "tensor"),
            P(None, "tensor"),
            P(None, "tensor"),
            P("tensor"),
            P("tensor"),
            P(),
            P("tensor", None),
            P(),
            P(None, "tensor"),
            P(None, "tensor"),
            P("tensor", None),
        ),
        check_vma=False,
    )
```
